256 devices in a mesh: gx: 8 (over y, core), gy: 32 (over z, x).
Axes of the slice: x: 4, y: 4, z: 8, core: 2. Of those that a mesh axis runs over, the one named last changes fastest.
Arguments:
- mesh_element_matrix: bfloat16 [262144, 256], P(('gx', 'gy')), may hold values from -12 to 12
- occupied_element_tally: int32 [256], P(('gx', 'gy')), may hold values from 1 to 1024, as said below
- transfer_assignment: int32 [256, 8], P(('gx', 'gy')), may hold values from -1 to 31, as said below
- adjoint_output: bfloat16 [131072, 256], P(('gx', 'gy')), may hold values from -6 to 6
- normalizer_factor: float32 [256], replicated, may hold values from 0.5 to 1.5
- entrance_matrix: bfloat16 [256, 512], replicated, may hold values from -0.375 to 0.375
- portion_matrix: bfloat16 [32, 64], replicated, may hold values from -80 to 80
- softness_matrix: bfloat16 [32], replicated, may hold values from -0.59765625 to 0.59765625
- default_softness: float32 [8], replicated, may hold values from 0.3 to 1.2
- request_matrix: float32 [32, 32], replicated, may hold values from -10 to 10
- lookup_matrix: float32 [32, 32], replicated, may hold values from -10 to 10
- content_matrix: float32 [32, 32], replicated, may hold values from -1 to 1
- exit_matrix: bfloat16 [256, 256], replicated, may hold values from -0.375 to 0.375
Outputs:
- result_bal: bfloat16 [131072, 256], P(('gx', 'gy'))
- cell_grad: bfloat16 [262144, 256], P(('gx', 'gy'))
- grad_in: float32 [256, 512], replicated
- grad_out: float32 [256, 256], replicated
- grad_slice: float32 [32, 64], replicated
The draws below stay inside these ranges and needn't reach their ends.
Inputs may be any that keep to these rules, and one draw needn't show every extreme that they name: `occupied_element_tally`: every device holds at least one live cell in its first rows; in every gx row some device is full. transfer_assignment[p, s] is -1 exactly when block s of device p has no live row; otherwise it is a gy index in the gx row of p. No device sends more than 1 block to one device, none receives more than 4 blocks, and both bounds are reached in every draw.
All inputs are finite; a program needn't handle non-finite values.
Results may differ from the reference program's by a relative error of at most 0.015.
The reference program's roundings to bfloat16 on the way count: a program that leaves them out, or rounds other values in their place, can miss the bound.
Values may be sent and summed in bfloat16 or wider, within the bound.
No kernel may reach another device: no remote copies, remote signals or barrier semaphores. Data moves between devices by JAX's collectives and lax.ppermute only.
A program may use at most 64 MiB of HBM per device.

```python
import math
import jax
import jax.numpy as jnp
from jax import lax

C = 256
FOCUS_GROUPS = 8
GROUP_PARTITIONS = 64
GROUP_WIDTH = 32
BLK = 128
SIN = 8
SOUT = 4
CELLS = 262144
BAL = 131072
N_GX = 8
N_GY = 32


def layout_draw(key):
    row_keys = jax.random.split(key, N_GX)

    def one_row(row_key):
        pair_key, shift_key, tail_key, receiver_key, offset_key = jax.random.split(row_key, 5)
        pairing = jax.random.permutation(pair_key, N_GY)
        shifts = jax.random.randint(shift_key, (N_GY // 2,), 0, SOUT - 1)
        first_held = (SOUT - 1 + shifts).at[0].set(SIN)
        second_held = (SOUT - 1 - shifts).at[0].set(1)
        paired = jnp.stack([first_held, second_held], axis=1).reshape(N_GY).astype(jnp.int32)
        blocks_held = jnp.zeros((N_GY,), jnp.int32).at[pairing].set(paired)
        tail_rows = jax.random.randint(tail_key, (N_GY,), 1, BLK + 1).at[pairing[0]].set(BLK)
        cell_count = (blocks_held - 1) * BLK + tail_rows
        start_block = jnp.cumsum(blocks_held) - blocks_held
        block_index = jnp.arange(SIN, dtype=jnp.int32)
        sequence = start_block[:, None] + block_index[None, :]
        receivers = jax.random.permutation(receiver_key, N_GY)
        offset = jax.random.randint(offset_key, (), 0, N_GY)
        target = receivers[(sequence + offset) % N_GY]
        target = jnp.where(block_index[None, :] < blocks_held[:, None], target, -1)
        return (cell_count.astype(jnp.int32), target.astype(jnp.int32))
    cell_count, target = jax.vmap(one_row)(row_keys)
    return (cell_count.reshape(N_GX * N_GY), target.reshape(N_GX * N_GY, SIN))


def draw_occupied_element_tally(key, part):
    return layout_draw(key)[0]


def draw_transfer_assignment(key, part):
    return layout_draw(key)[1]


def draw_mesh_element_matrix(key, part):
    key = jax.random.fold_in(key, 21)
    device_key, block_key, jitter_key = jax.random.split(key, 3)
    device_total = CELLS // (SIN * BLK)
    device_base = jax.random.normal(device_key, (device_total, C), jnp.float32)
    block_base = jax.random.normal(block_key, (CELLS // BLK, C), jnp.float32)
    row_device = jnp.arange(CELLS) // (SIN * BLK)
    row_block = jnp.arange(CELLS) // BLK
    jitter = jax.random.normal(jitter_key, (CELLS, C), jnp.float32)
    values = 1.5 * device_base[row_device] + 0.8 * block_base[row_block] + jitter
    return jnp.clip(values, -12.0, 12.0).astype(jnp.bfloat16)


def draw_portion_matrix(key, part):
    key = jax.random.fold_in(key, 31)
    spread_key = jax.random.fold_in(key, 0)
    spread = jax.random.normal(spread_key, (GROUP_WIDTH, GROUP_PARTITIONS), jnp.float32) * (2.0 / math.sqrt(GROUP_WIDTH))
    return jnp.clip(spread, -80.0, 80.0).astype(jnp.bfloat16)


def draw_request_matrix(key, part):
    key = jax.random.fold_in(key, 41)
    values = jax.random.normal(key, (GROUP_WIDTH, GROUP_WIDTH), jnp.float32) / math.sqrt(GROUP_WIDTH)
    return jnp.clip(values, -10.0, 10.0)


def draw_lookup_matrix(key, part):
    key = jax.random.fold_in(key, 42)
    values = jax.random.normal(key, (GROUP_WIDTH, GROUP_WIDTH), jnp.float32) / math.sqrt(GROUP_WIDTH)
    return jnp.clip(values, -10.0, 10.0)


def steps_of(own_key, dims, shards, least, top_value):
    def one(axis_at, parts):
        draws = jax.random.uniform(jax.random.fold_in(jax.random.fold_in(own_key, 6), axis_at), (parts,), jnp.float32, least / len(shards), top_value / len(shards))
        return jnp.repeat(jnp.exp(draws), dims[axis_at] // parts).reshape((-1,) + (1,) * (len(dims) - axis_at - 1))

    gain = one(*shards[0])
    for cut in shards[1:]:
        gain = gain * one(*cut)
    return gain


def scatter_about(rng, extent, width, reach, cuts=(), held_as=jnp.bfloat16):
    array = width * jax.random.normal(rng, extent, jnp.float32)
    if cuts:
        array = array * steps_of(rng, extent, cuts, -0.22, 0.18)
    return jnp.clip(array, -reach, reach).astype(held_as)


def setup_inputs(seed: int = 0) -> dict:
    key_of = jax.random.split(jax.random.key(seed), 14)
    mesh_element_matrix = draw_mesh_element_matrix(jax.random.fold_in(key_of[13], 71), 0)
    occupied_element_tally = draw_occupied_element_tally(jax.random.fold_in(key_of[13], 71), 0)
    transfer_assignment = draw_transfer_assignment(jax.random.fold_in(key_of[13], 71), 0)
    adjoint_output = scatter_about(key_of[3], (BAL, C), 1.0, 6.0, ((0, 256),))
    normalizer_factor = jnp.clip(jax.random.uniform(key_of[4], (C,), jnp.float32, 0.5, 1.5), 0.5, 1.5)
    entrance_matrix = scatter_about(key_of[5], (C, 2 * C), C ** -0.5, 0.375)
    portion_matrix = draw_portion_matrix(jax.random.fold_in(key_of[13], 71), 0)
    softness_matrix = scatter_about(key_of[7], (GROUP_WIDTH,), 0.1, 0.59765625)
    default_softness = jnp.clip(jnp.exp(jax.random.uniform(key_of[8], (FOCUS_GROUPS,), jnp.float32, math.log(0.3), math.log(1.2))), 0.3, 1.2)
    request_matrix = draw_request_matrix(jax.random.fold_in(key_of[13], 71), 0)
    lookup_matrix = draw_lookup_matrix(jax.random.fold_in(key_of[13], 71), 0)
    content_matrix = scatter_about(key_of[11], (GROUP_WIDTH, GROUP_WIDTH), GROUP_WIDTH ** -0.5, 1.0, (), jnp.float32)
    exit_matrix = scatter_about(key_of[12], (C, C), C ** -0.5, 0.375)
    return dict(mesh_element_matrix=mesh_element_matrix, occupied_element_tally=occupied_element_tally, transfer_assignment=transfer_assignment, adjoint_output=adjoint_output, normalizer_factor=normalizer_factor, entrance_matrix=entrance_matrix, portion_matrix=portion_matrix, softness_matrix=softness_matrix, default_softness=default_softness, request_matrix=request_matrix, lookup_matrix=lookup_matrix, content_matrix=content_matrix, exit_matrix=exit_matrix)


norm_eps = 1e-05
slice_eps = 1e-05

def block_map(occupied_element_tally, transfer_assignment):
    block_index = jnp.arange(SIN, dtype=jnp.int32)
    block_rows = jnp.clip(occupied_element_tally[:, None] - block_index[None, :] * BLK, 0, BLK).astype(jnp.int32)
    target_gy = transfer_assignment.reshape(N_GX, N_GY * SIN)
    receivers = jnp.arange(N_GY, dtype=jnp.int32)
    onehot_hits = (target_gy[:, :, None] == receivers[None, None, :]).astype(jnp.int32)
    arrival_order = jnp.cumsum(onehot_hits, axis=1) - 1
    arrival_slot = lax.optimization_barrier(jnp.sum(arrival_order * onehot_hits, axis=-1))
    row_of_gx = jnp.arange(N_GX, dtype=jnp.int32)[:, None]
    bal_slot = (row_of_gx * N_GY + target_gy) * SOUT + arrival_slot
    bal_slot = jnp.where(target_gy >= 0, bal_slot, N_GX * N_GY * SOUT).astype(jnp.int32)
    return (bal_slot.reshape(-1), block_rows.reshape(-1))

def norm_rows(cells_rows, normalizer_factor):
    cells_f32 = cells_rows.astype(jnp.float32)
    row_mean = lax.optimization_barrier(jnp.mean(cells_f32, axis=-1, keepdims=True))
    centered = cells_f32 - row_mean
    variance = lax.optimization_barrier(jnp.mean(centered * centered, axis=-1, keepdims=True))
    inv_std = lax.rsqrt(variance + norm_eps)
    unit_rows = centered * inv_std
    standardized = (unit_rows * normalizer_factor[None, :]).astype(jnp.bfloat16)
    return (cells_f32, unit_rows, inv_std, standardized)

def portion_membership(mapped_elements, entry_alive_flags, portion_matrix, softness_matrix, default_softness):
    entry_accumulated = mapped_elements.shape[0]
    mesh_entries = mapped_elements[:, :C].reshape(entry_accumulated, FOCUS_GROUPS, GROUP_WIDTH)
    interior_entries = mapped_elements[:, C:].reshape(entry_accumulated * FOCUS_GROUPS, GROUP_WIDTH)
    portion_affinity = jnp.dot(interior_entries, portion_matrix, preferred_element_type=jnp.float32).reshape(entry_accumulated, FOCUS_GROUPS, GROUP_PARTITIONS)
    softness_presquash = jnp.dot(interior_entries, softness_matrix, preferred_element_type=jnp.float32).reshape(entry_accumulated, FOCUS_GROUPS)
    group_softness = default_softness[None, :] + jax.nn.softplus(softness_presquash)
    rescaled_affinity = portion_affinity / group_softness[:, :, None]
    portion_chance = jax.nn.softmax(rescaled_affinity, axis=-1)
    portion_lowprecision = (portion_chance * entry_alive_flags[:, None, None]).astype(jnp.bfloat16)
    return (mesh_entries, interior_entries, softness_presquash, group_softness, rescaled_affinity, portion_chance, portion_lowprecision)

def token_forward(numerator, denominator, request_matrix, lookup_matrix, content_matrix):
    upper_value = lax.Precision.HIGHEST
    slice_tokens = numerator / (denominator[:, :, None] + slice_eps)
    query_rows = jnp.einsum('woy,yu->wou', slice_tokens, request_matrix, precision=upper_value)
    projected_keys = jnp.einsum('woy,yu->wou', slice_tokens, lookup_matrix, precision=upper_value)
    projected_values = jnp.einsum('woy,yu->wou', slice_tokens, content_matrix, precision=upper_value)
    scores = jnp.einsum('hme,hne->hmn', query_rows, projected_keys, precision=upper_value) * GROUP_WIDTH ** (-0.5)
    attention = jax.nn.softmax(scores, axis=-1)
    mixed = jnp.einsum('hmn,hne->hme', attention, projected_values, precision=upper_value)
    return (slice_tokens, query_rows, projected_keys, projected_values, attention, mixed.astype(jnp.bfloat16))

def token_backward(tok_grad_sum, token_state, denominator, request_matrix, lookup_matrix, content_matrix):
    upper_value = lax.Precision.HIGHEST
    slice_tokens, query_rows, projected_keys, projected_values, attention, mixed_half_float = token_state
    grad_att = jnp.einsum('hme,hne->hmn', tok_grad_sum, projected_values, precision=upper_value)
    value_gradient = jnp.einsum('hmn,hme->hne', attention, tok_grad_sum, precision=upper_value)
    grad_scores = attention * (grad_att - lax.optimization_barrier(jnp.sum(attention * grad_att, axis=-1, keepdims=True))) * GROUP_WIDTH ** (-0.5)
    query_gradient = jnp.einsum('hmn,hne->hme', grad_scores, projected_keys, precision=upper_value)
    key_gradient = jnp.einsum('hmn,hme->hne', grad_scores, query_rows, precision=upper_value)
    token_gradient = jnp.einsum('fgs,js->fgj', query_gradient, request_matrix, precision=upper_value)
    token_gradient = token_gradient + jnp.einsum('fgs,js->fgj', key_gradient, lookup_matrix, precision=upper_value)
    token_gradient = token_gradient + jnp.einsum('fgs,js->fgj', value_gradient, content_matrix, precision=upper_value)
    inverse = 1.0 / (denominator + slice_eps)
    numerator_gradient = (token_gradient * inverse[:, :, None]).astype(jnp.bfloat16)
    denominator_gradient = -lax.optimization_barrier(jnp.sum(token_gradient * slice_tokens, axis=-1)) * inverse
    return (numerator_gradient, denominator_gradient)

def deslice_rows(portion_lowprecision, mixed_half_float):
    entry_accumulated = portion_lowprecision.shape[0]
    merged_heads = jnp.einsum('ngx,gxw->ngw', portion_lowprecision.astype(jnp.float32), mixed_half_float.astype(jnp.float32))
    return merged_heads.astype(jnp.bfloat16).reshape(entry_accumulated, C)

def cot_first(cot_rows, entry_alive_flags, mixed_half_float, exit_matrix, portion_lowprecision):
    entry_accumulated = cot_rows.shape[0]
    masked_cot = jnp.where(entry_alive_flags[:, None] > 0, cot_rows, jnp.zeros_like(cot_rows))
    unslice_gradient = jnp.dot(masked_cot, exit_matrix.T, preferred_element_type=jnp.float32).astype(jnp.bfloat16).reshape(entry_accumulated, FOCUS_GROUPS, GROUP_WIDTH)
    token_gradient_partial = jnp.einsum('ajq,ajs->jqs', portion_lowprecision.astype(jnp.float32), unslice_gradient.astype(jnp.float32))
    probability_gradient_first = jnp.einsum('bco,cfo->bcf', unslice_gradient.astype(jnp.float32), mixed_half_float.astype(jnp.float32))
    return (masked_cot, unslice_gradient, token_gradient_partial, probability_gradient_first)

def reference(mesh_element_matrix, occupied_element_tally, transfer_assignment, adjoint_output, normalizer_factor, entrance_matrix, portion_matrix, softness_matrix, default_softness, request_matrix, lookup_matrix, content_matrix, exit_matrix):
    bal_slot, block_rows = block_map(occupied_element_tally, transfer_assignment)
    devices_all = N_GX * N_GY
    bal_blocks = devices_all * SOUT
    dev_rows = SOUT * BLK
    cells_bal = jnp.zeros((bal_blocks, BLK, C), jnp.bfloat16).at[bal_slot].set(mesh_element_matrix.reshape(devices_all * SIN, BLK, C), mode='drop')
    rows_bal = jnp.zeros((bal_blocks,), jnp.int32).at[bal_slot].set(block_rows, mode='drop')
    mask_bal = (jnp.arange(BLK, dtype=jnp.int32)[None, :] < rows_bal[:, None]).astype(jnp.float32)
    cells_dev = cells_bal.reshape(devices_all, dev_rows, C)
    mask_dev = mask_bal.reshape(devices_all, dev_rows)
    cot_dev = adjoint_output.reshape(devices_all, dev_rows, C)

    def first_pass(carry, item):
        cells_rows, entry_alive_flags = item
        standardized = norm_rows(cells_rows, normalizer_factor)[3]
        mapped_elements = jnp.dot(standardized, entrance_matrix, preferred_element_type=jnp.float32).astype(jnp.bfloat16)
        assignment_chance = portion_membership(mapped_elements, entry_alive_flags, portion_matrix, softness_matrix, default_softness)
        mesh_entries = assignment_chance[0].astype(jnp.float32)
        slice_single_float = assignment_chance[6].astype(jnp.float32)
        numerator_partial = jnp.einsum('ajq,ajs->jqs', slice_single_float, mesh_entries)
        denom_part = lax.optimization_barrier(jnp.sum(slice_single_float, axis=0))
        return ((carry[0] + numerator_partial, carry[1] + denom_part), mapped_elements)
    start_sums = (jnp.zeros((FOCUS_GROUPS, GROUP_PARTITIONS, GROUP_WIDTH), jnp.float32), jnp.zeros((FOCUS_GROUPS, GROUP_PARTITIONS), jnp.float32))
    (numerator, denominator), projected_dev = lax.scan(first_pass, start_sums, (cells_dev, mask_dev))
    token_state = token_forward(numerator, denominator, request_matrix, lookup_matrix, content_matrix)
    mixed_half_float = token_state[5]

    def second_pass(carry, item):
        cells_rows, entry_alive_flags, mapped_elements, cot_rows = item
        cells_f32 = cells_rows.astype(jnp.float32)
        portion_lowprecision = portion_membership(mapped_elements, entry_alive_flags, portion_matrix, softness_matrix, default_softness)[6]
        deslice_bf = deslice_rows(portion_lowprecision, mixed_half_float)
        branch_out = jnp.dot(deslice_bf, exit_matrix, preferred_element_type=jnp.float32)
        result_rows = (entry_alive_flags[:, None] * (cells_f32 + branch_out)).astype(jnp.bfloat16)
        masked_cot, unslice_gradient, token_gradient_partial, probability_gradient_first = cot_first(cot_rows, entry_alive_flags, mixed_half_float, exit_matrix, portion_lowprecision)
        out_grad_part = jnp.dot(deslice_bf.T, masked_cot, preferred_element_type=jnp.float32)
        return ((carry[0] + token_gradient_partial, carry[1] + out_grad_part), result_rows)
    start_grads = (jnp.zeros((FOCUS_GROUPS, GROUP_PARTITIONS, GROUP_WIDTH), jnp.float32), jnp.zeros((C, C), jnp.float32))
    (tok_grad_sum, out_grad_sum), result_dev = lax.scan(second_pass, start_grads, (cells_dev, mask_dev, projected_dev, cot_dev))
    numerator_gradient, denominator_gradient = token_backward(tok_grad_sum, token_state, denominator, request_matrix, lookup_matrix, content_matrix)

    def third_pass(carry, item):
        cells_rows, entry_alive_flags, mapped_elements, cot_rows = item
        entry_accumulated = cells_rows.shape[0]
        cells_f32, unit_rows, inv_std, standardized = norm_rows(cells_rows, normalizer_factor)
        mesh_entries, interior_entries, softness_presquash, group_softness, rescaled_affinity, portion_chance, portion_lowprecision = portion_membership(mapped_elements, entry_alive_flags, portion_matrix, softness_matrix, default_softness)
        masked_cot, unslice_gradient, token_gradient_partial, probability_gradient_first = cot_first(cot_rows, entry_alive_flags, mixed_half_float, exit_matrix, portion_lowprecision)
        numerator_single_float = numerator_gradient.astype(jnp.float32)
        probability_gradient = probability_gradient_first + jnp.einsum('bco,cfo->bcf', mesh_entries.astype(jnp.float32), numerator_single_float) + denominator_gradient[None, :, :]
        probability_gradient = probability_gradient * entry_alive_flags[:, None, None]
        feature_gradient = jnp.einsum('ngx,gxw->ngw', portion_lowprecision.astype(jnp.float32), numerator_single_float)
        rescaled_adjoint = portion_chance * (probability_gradient - lax.optimization_barrier(jnp.sum(portion_chance * probability_gradient, axis=-1, keepdims=True)))
        affinity_adjoint = (rescaled_adjoint / group_softness[:, :, None]).astype(jnp.bfloat16).reshape(entry_accumulated * FOCUS_GROUPS, GROUP_PARTITIONS)
        softness_adjoint = -lax.optimization_barrier(jnp.sum(rescaled_adjoint * rescaled_affinity, axis=-1)) / group_softness * jax.nn.sigmoid(softness_presquash)
        adjoint_between = jnp.dot(affinity_adjoint, portion_matrix.T, preferred_element_type=jnp.float32)
        adjoint_between = adjoint_between + softness_adjoint.reshape(entry_accumulated * FOCUS_GROUPS, 1) * softness_matrix.astype(jnp.float32)[None, :]
        slice_grad_part = jnp.dot(interior_entries.T, affinity_adjoint, preferred_element_type=jnp.float32)
        grad_proj = jnp.concatenate([feature_gradient.reshape(entry_accumulated, C), adjoint_between.reshape(entry_accumulated, C)], axis=1).astype(jnp.bfloat16)
        in_grad_part = jnp.dot(standardized.T, grad_proj, preferred_element_type=jnp.float32)
        grad_normed = jnp.dot(grad_proj, entrance_matrix.T, preferred_element_type=jnp.float32)
        grad_unit = grad_normed * normalizer_factor[None, :]
        grad_norm_in = inv_std * (grad_unit - lax.optimization_barrier(jnp.mean(grad_unit, axis=-1, keepdims=True)) - unit_rows * lax.optimization_barrier(jnp.mean(grad_unit * unit_rows, axis=-1, keepdims=True)))
        cell_grad = (masked_cot.astype(jnp.float32) + grad_norm_in).astype(jnp.bfloat16)
        return ((carry[0] + in_grad_part, carry[1] + slice_grad_part), cell_grad)
    start_weights = (jnp.zeros((C, 2 * C), jnp.float32), jnp.zeros((GROUP_WIDTH, GROUP_PARTITIONS), jnp.float32))
    (in_grad_sum, slice_grad_sum), grad_dev = lax.scan(third_pass, start_weights, (cells_dev, mask_dev, projected_dev, cot_dev))
    grad_scale = 1.0 / math.sqrt(CELLS)
    cell_grad = jnp.take(grad_dev.reshape(bal_blocks, BLK, C), bal_slot, axis=0, mode='fill', fill_value=0).reshape(CELLS, C)
    result_bal = result_dev.reshape(BAL, C)
    return (result_bal, cell_grad, in_grad_sum * grad_scale, out_grad_sum * grad_scale, slice_grad_sum * grad_scale)
```

```python
import math

import jax
import jax.numpy as jnp
from jax import lax
from jax.experimental import pallas as pl
from jax.experimental.pallas import tpu as pltpu
from jax.sharding import Mesh, PartitionSpec as P

C = 256
HEADS = 8
SLICES = 64
WIDTH = 32
BLK = 128
SIN = 8
SOUT = 4
GX = 8
GY = 32
PIECE = BLK // GY
ROWS = GY * SOUT * PIECE
HOME = GY * SIN * PIECE
SEND = (SIN + SOUT) * PIECE
GROUP = 4 * SEND
META = 16
TOKEN_ROWS = 40
MIX_ROWS = 48
GRAD_ROWS = 56

norm_eps = 1e-05
slice_eps = 1e-05

F32 = jnp.float32
BF16 = jnp.bfloat16
HI = lax.Precision.HIGHEST
NN = (((1,), (0,)), ((), ()))
NT = (((1,), (1,)), ((), ()))
TN = (((0,), (0,)), ((), ()))


def mm(a, b, dims=NN, precision=None):
    return lax.dot_general(a, b, dims, precision=precision, preferred_element_type=F32)


def iota(shape, dim):
    return lax.broadcasted_iota(jnp.int32, shape, dim)


def call(body, outs, *args, scalars=0, scratch=(), flops=0, vmem=40):
    vm = pl.BlockSpec(memory_space=pltpu.VMEM)
    sm = pl.BlockSpec(memory_space=pltpu.SMEM)
    single = not isinstance(outs, (list, tuple))
    listed = [outs] if single else list(outs)
    moved = sum(math.prod(a.shape) * a.dtype.itemsize for a in list(args) + listed)
    res = pl.pallas_call(
        body,
        out_shape=listed,
        in_specs=[sm] * scalars + [vm] * (len(args) - scalars),
        out_specs=[vm] * len(listed),
        scratch_shapes=list(scratch),
        compiler_params=pltpu.CompilerParams(vmem_limit_bytes=vmem * 2**20),
        cost_estimate=pl.CostEstimate(flops=flops, bytes_accessed=moved, transcendentals=0),
    )(*args)
    return res[0] if single else res


def sds(shape, dtype):
    return jax.ShapeDtypeStruct(shape, dtype)


def column(row):
    n = row.shape[1]
    return jnp.sum(jnp.where(iota((n, n), 0) == iota((n, n), 1), row, 0.0), axis=1, keepdims=True)


def piece_order(back):
    sent = iota((GROUP, GROUP), 1 if back else 0)
    kept = iota((GROUP, GROUP), 0 if back else 1)
    part = (
        (sent >= SEND).astype(jnp.int32)
        + (sent >= 2 * SEND).astype(jnp.int32)
        + (sent >= 3 * SEND).astype(jnp.int32)
    )
    within = sent - part * SEND
    source = (within >> 2) * 16 + part * PIECE + (within & 3)
    return (source == kept).astype(F32).astype(BF16)


def pack_kernel(tally, plan, cells, cot, out):
    order = piece_order(False)
    for j in range(8):
        at = 16 * j
        rows = [cells[s * BLK + at : s * BLK + at + 16, :] for s in range(SIN)]
        rows += [cot[t * BLK + at : t * BLK + at + 16, :] for t in range(SOUT)]
        moved = mm(order, jnp.concatenate(rows, axis=0)).astype(BF16)
        for a in range(4):
            out[4 * j + a, 0:SEND, :] = moved[a * SEND : (a + 1) * SEND]
    block = iota((META, C), 1) >> 2
    target = jnp.zeros((META, C), jnp.int32)
    for s in range(SIN):
        target = jnp.where(block == s, plan[0, s], target)
    held = jnp.clip(tally[0] - block * BLK, 0, BLK)
    meta = jnp.where(iota((META, C), 0) < 8, target, held).astype(F32).astype(BF16)
    for j in range(GY):
        out[j, SEND : SEND + META, :] = meta


def unpack_kernel(recv, result, cell_grad):
    order = piece_order(True)
    for j in range(8):
        at = 16 * j
        rows = jnp.concatenate([recv[4 * j + a] for a in range(4)], axis=0)
        moved = mm(order, rows).astype(BF16)
        for s in range(SIN):
            cell_grad[s * BLK + at : s * BLK + at + 16, :] = moved[s * 16 : s * 16 + 16]
        for t in range(SOUT):
            u = SIN + t
            result[t * BLK + at : t * BLK + at + 16, :] = moved[u * 16 : u * 16 + 16]


def forward_kernel(
    spot, recv, gain, entrance, portion, softness, base, exit_w,
    token, pick, xt_out, normed_out, proj_out, prob_out, scaled_out, slice_out,
    uns_out, cot_out, rows_out, heads_out, spread_out,
):
    mine = spot[0]
    cells = recv[:, 0 : SIN * PIECE, :].reshape(HOME, C)
    cot = recv[:, SIN * PIECE : SEND, :].reshape(ROWS, C)
    meta = recv[:, SEND : SEND + META, 0:128].astype(F32)
    target = jnp.max(meta[:, 0:8, :], axis=1)
    held = jnp.max(meta[:, 8:16, :], axis=1)

    lane = iota((GY, 128), 1)
    lane_f = lane.astype(F32)
    hits = [(target[:, 4 * s : 4 * s + 1] == lane_f).astype(F32) for s in range(SIN)]
    taken = hits[0]
    for s in range(1, SIN):
        taken = taken + hits[s]
    before = (iota((GY, GY), 1) < iota((GY, GY), 0)).astype(F32).astype(BF16)
    place = mm(before, taken.astype(BF16)) + lane_f * SOUT + 1.0
    dest = jnp.zeros((GY, 128), F32)
    for s in range(SIN):
        found = jnp.sum(hits[s] * place, axis=1, keepdims=True)
        dest = jnp.where((lane >> 2) == s, found, dest)
    row_in_block = (mine * PIECE + (lane & 3)).astype(F32)
    dest = jnp.where(row_in_block < held, dest, 0.0) - 1.0
    repeat = ((iota((HOME, GY), 0) >> 5) == iota((HOME, GY), 1)).astype(F32).astype(BF16)
    wide = mm(repeat, dest.astype(BF16))
    own = iota((HOME, 128), 1) == (iota((HOME, 128), 0) & 31)
    dest_col = jnp.sum(jnp.where(own, wide, 0.0), axis=1, keepdims=True)
    k_col = (iota((HOME, 1), 0) & 3).astype(F32)
    spot_col = (dest_col * 4.0 + k_col).astype(jnp.int32)
    pick[...] = (spot_col == iota((HOME, ROWS), 1)).astype(F32).astype(BF16)
    live = mm(jnp.ones((8, HOME), BF16), pick[...])[0:1, :]

    xt = mm(cells, pick[...], TN)
    xt_out[...] = xt.astype(BF16)
    mean = jnp.sum(xt, axis=0, keepdims=True) * (1.0 / C)
    centered = xt - mean
    var = jnp.sum(centered * centered, axis=0, keepdims=True) * (1.0 / C)
    inv = lax.rsqrt(var + norm_eps)
    gain_col = column(gain[...])
    normed = (centered * inv * gain_col).astype(BF16)
    normed_out[...] = normed
    proj_out[...] = mm(entrance[...], normed, TN).astype(BF16)
    rows_out[0:1, :] = live
    rows_out[1:2, :] = mean
    rows_out[2:3, :] = inv

    tall = ((iota((C, WIDTH), 0) & 31) == iota((C, WIDTH), 1)).astype(F32).astype(BF16)
    broad = ((iota((SLICES, 512), 1) & 63) == iota((SLICES, 512), 0)).astype(F32).astype(BF16)
    spread = mm(mm(tall, portion[...]).astype(BF16), broad)
    same = (iota((C, 512), 0) >> 5) == (iota((C, 512), 1) >> 6)
    spread_out[...] = jnp.where(same, spread, 0.0).astype(BF16)
    soft_row = mm(softness[...], tall, NT)
    soft_same = (iota((HEADS, C), 1) >> 5) == iota((HEADS, C), 0)
    soft_spread = jnp.where(soft_same, soft_row, 0.0).astype(BF16)

    mid = proj_out[C : 2 * C, :]
    presq = mm(soft_spread, mid)
    softplus = jnp.maximum(presq, 0.0) + jnp.log1p(jnp.exp(-jnp.abs(presq)))
    inv_temp = 1.0 / (column(base[...]) + softplus)
    heads_out[0:8, :] = inv_temp
    heads_out[8:16, :] = presq
    scaled_out[...] = mm(spread_out[...], mid, TN)

    back = mm(exit_w[...], cot, NT) * live
    uns_out[...] = back.astype(BF16)
    eye = (iota((C, C), 0) == iota((C, C), 1)).astype(F32).astype(BF16)
    cot_out[...] = (mm(eye, cot, NT) * live).astype(BF16)

    for h in range(HEADS):
        at = h * SLICES
        scaled = scaled_out[at : at + SLICES, :] * inv_temp[h : h + 1, :]
        scaled_out[at : at + SLICES, :] = scaled
        top = jnp.max(scaled, axis=0, keepdims=True)
        e = jnp.exp(scaled - top)
        prob = e * (1.0 / jnp.sum(e, axis=0, keepdims=True))
        prob_out[at : at + SLICES, :] = prob
        half = (prob * live).astype(BF16)
        slice_out[at : at + SLICES, :] = half
        left = jnp.concatenate(
            [
                proj_out[h * WIDTH : (h + 1) * WIDTH, :],
                uns_out[h * WIDTH : (h + 1) * WIDTH, :],
                jnp.ones((16, ROWS), BF16),
            ],
            axis=0,
        )
        sums = mm(left, half, NT)
        token[h, 0:WIDTH, 0:SLICES] = sums[0:WIDTH]
        token[h, 0:WIDTH, SLICES:128] = sums[WIDTH : 2 * WIDTH]
        token[h, WIDTH:TOKEN_ROWS, 0:SLICES] = sums[2 * WIDTH : 2 * WIDTH + 8]
        token[h, WIDTH:TOKEN_ROWS, SLICES:128] = jnp.zeros((8, SLICES), F32)


def spread_kernel(recv, out):
    n = recv.shape[0]
    total = recv[0].astype(F32)
    for i in range(1, n):
        total = total + recv[i].astype(F32)
    total = total.astype(out.dtype)
    for i in range(out.shape[0]):
        out[i] = total


def spread_sum(recv, copies, dtype):
    return call(spread_kernel, sds((copies,) + recv.shape[1:], dtype), recv)


def token_kernel(recv, request, lookup, content, out):
    total = recv[0].astype(F32)
    for i in range(1, GY):
        total = total + recv[i].astype(F32)
    inverse = 1.0 / (total[WIDTH : WIDTH + 1, 0:SLICES] + slice_eps)
    tok = total[0:WIDTH, 0:SLICES] * inverse
    cot = total[0:WIDTH, SLICES:128]
    scale = WIDTH ** (-0.5)
    q = mm(request[...], tok, TN, HI)
    k = mm(lookup[...], tok, TN, HI)
    v = mm(content[...], tok, TN, HI)
    scores = mm(k, q, TN, HI) * scale
    e = jnp.exp(scores - jnp.max(scores, axis=0, keepdims=True))
    att = e / jnp.sum(e, axis=0, keepdims=True)
    mixed = mm(v, att, NN, HI)
    g_att = mm(v, cot, TN, HI)
    g_v = mm(cot, att, NT, HI)
    g_s = att * (g_att - jnp.sum(att * g_att, axis=0, keepdims=True)) * scale
    g_q = mm(k, g_s, NN, HI)
    g_k = mm(q, g_s, NT, HI)
    g_tok = mm(request[...], g_q, NN, HI)
    g_tok = g_tok + mm(lookup[...], g_k, NN, HI)
    g_tok = g_tok + mm(content[...], g_v, NN, HI)
    g_num = g_tok * inverse
    g_den = -jnp.sum(g_tok * tok, axis=0, keepdims=True) * inverse
    g_den_hi = g_den.astype(BF16).astype(F32)
    g_den_lo = g_den - g_den_hi
    main = jnp.concatenate([mixed, g_num], axis=1).astype(BF16)
    tail = jnp.concatenate([g_den_hi, g_den_lo], axis=1)
    tail = jnp.broadcast_to(tail, (16, 128)).astype(BF16)
    for i in range(GX):
        out[i, 0:WIDTH, :] = main
        out[i, WIDTH:MIX_ROWS, :] = tail


def backward_kernel(
    mix, gain, entrance, softness, exit_w,
    pick, xt_in, normed_in, proj_in, prob_in, scaled_in, slice_in,
    uns_in, cot_in, rows_in, heads_in, spread_in,
    send, grads, weave, stack, gprob, affs, gproj,
):
    live = rows_in[0:1, :]
    mean = rows_in[1:2, :]
    inv = rows_in[2:3, :]
    weave[...] = jnp.zeros_like(weave)
    lane = iota((WIDTH, 128), 1)
    lane16 = iota((16, 128), 1)
    sub16 = iota((16, 128), 0)
    for h in range(HEADS):
        block = mix[h].astype(F32)
        turned = pltpu.roll(block, SLICES, 1)
        low = h % 2 == 0
        left, right = (block, turned) if low else (turned, block)
        here = (lane < SLICES) if low else (lane >= SLICES)
        at = (h // 2) * 128
        weave[h * WIDTH : (h + 1) * WIDTH, at : at + 128] = jnp.where(
            here, left[0:WIDTH], 0.0
        ).astype(BF16)
        weave[C + h * WIDTH : C + (h + 1) * WIDTH, at : at + 128] = jnp.where(
            here, right[0:WIDTH], 0.0
        ).astype(BF16)
    for g in range(HEADS // 2):
        even = mix[2 * g, WIDTH:MIX_ROWS, :].astype(F32)
        odd = mix[2 * g + 1, WIDTH:MIX_ROWS, :].astype(F32)
        upper = jnp.where(lane16 < SLICES, even, pltpu.roll(odd, SLICES, 1))
        lower = jnp.where(lane16 < SLICES, pltpu.roll(even, SLICES, 1), odd)
        both = jnp.where(sub16 == 0, upper, jnp.where(sub16 == 1, lower, 0.0))
        weave[2 * C : 2 * C + 16, g * 128 : (g + 1) * 128] = both.astype(BF16)
    stack[0:C, :] = uns_in[...]
    stack[C : 2 * C, :] = proj_in[0:C, :]
    stack[2 * C : 2 * C + 16, :] = jnp.ones((16, ROWS), BF16)

    rows = mm(weave[0 : 2 * C, :], slice_in[...])
    deslice = rows[0:C].astype(BF16)
    gproj[0:C, :] = rows[C : 2 * C].astype(BF16)
    gprob[...] = mm(weave[...], stack[...], TN)
    branch = mm(exit_w[...], deslice, TN)
    xt = xt_in[...].astype(F32)
    result = (live * (xt + branch)).astype(BF16)
    eye = (iota((ROWS, ROWS), 0) == iota((ROWS, ROWS), 1)).astype(F32).astype(BF16)
    result_rows = mm(eye, result, NT).astype(BF16)
    for q in range(GY):
        send[q, SIN * PIECE : SEND, :] = result_rows[q * 16 : (q + 1) * 16]
    out_grad = mm(deslice, cot_in[...], NT)
    for b in range(2):
        grads[(4 + b) * C : (5 + b) * C, :] = out_grad[:, b * 128 : (b + 1) * 128].astype(
            grads.dtype
        )

    softs = []
    for h in range(HEADS):
        at = h * SLICES
        inv_temp = heads_in[h : h + 1, :]
        presq = heads_in[8 + h : 9 + h, :]
        prob = prob_in[at : at + SLICES, :]
        gp = gprob[at : at + SLICES, :] * live
        adj = prob * (gp - jnp.sum(prob * gp, axis=0, keepdims=True))
        affs[at : at + SLICES, :] = (adj * inv_temp).astype(BF16)
        pulled = jnp.sum(adj * scaled_in[at : at + SLICES, :], axis=0, keepdims=True)
        softs.append(-pulled * inv_temp * (1.0 / (1.0 + jnp.exp(-presq))))
    between = mm(spread_in[...], affs[...])
    soft_col = column(softness[...].astype(F32))
    slice_grad = jnp.zeros((WIDTH, SLICES), F32)
    for h in range(HEADS):
        at = h * WIDTH
        part = between[at : at + WIDTH] + soft_col * softs[h]
        gproj[C + at : C + at + WIDTH, :] = part.astype(BF16)
        slice_grad = slice_grad + mm(
            proj_in[C + at : C + at + WIDTH, :], affs[h * SLICES : (h + 1) * SLICES, :], NT
        )
    in_grad = mm(normed_in[...], gproj[...], NT)
    for b in range(4):
        grads[b * C : (b + 1) * C, :] = in_grad[:, b * 128 : (b + 1) * 128].astype(grads.dtype)
    tail = jnp.concatenate([slice_grad, jnp.zeros((WIDTH, SLICES), F32)], axis=1)
    grads[6 * C : 6 * C + WIDTH, :] = tail.astype(grads.dtype)
    grads[6 * C + WIDTH :, :] = jnp.zeros((GY * GRAD_ROWS - 6 * C - WIDTH, 128), grads.dtype)

    g_unit = mm(entrance[...], gproj[...]) * column(gain[...])
    unit = (xt - mean) * inv
    m1 = jnp.sum(g_unit, axis=0, keepdims=True) * (1.0 / C)
    m2 = jnp.sum(g_unit * unit, axis=0, keepdims=True) * (1.0 / C)
    cell = cot_in[...].astype(F32) + inv * (g_unit - m1 - unit * m2)
    cell_rows = mm(pick[...], cell.astype(BF16), NT).astype(BF16)
    for q in range(GY):
        send[q, 0 : SIN * PIECE, :] = cell_rows[q * 32 : (q + 1) * 32]


def weight_kernel(scale, recv, grad_in, grad_out, grad_slice):
    def part(b):
        return recv[b * C : (b + 1) * C, :].astype(F32) * scale

    for b in range(4):
        grad_in[:, b * 128 : (b + 1) * 128] = part(b)
    for b in range(2):
        grad_out[:, b * 128 : (b + 1) * 128] = part(4 + b)
    grad_slice[...] = recv[6 * C : 6 * C + WIDTH, 0:SLICES].astype(F32) * scale


def shards(
    cells, tally, plan, cot, gain, entrance, portion, softness, base,
    request, lookup, content, exit_w,
):
    gain = gain.reshape(1, C)
    softness = softness.reshape(1, WIDTH)
    base = base.reshape(1, HEADS)
    scale = 1.0 / math.sqrt(GX * GY * SIN * BLK)

    def swap(x, axes):
        return lax.all_to_all(x, axes, 0, 0, tiled=True)

    sent = call(
        pack_kernel, sds((GY, SEND + META, C), BF16), tally, plan, cells, cot, scalars=2
    )
    recv = swap(sent, ("z", "x"))
    spot = (lax.axis_index("z") * 4 + lax.axis_index("x")).astype(jnp.int32).reshape(1)
    state = call(
        forward_kernel,
        [
            sds((HEADS, TOKEN_ROWS, 128), F32),
            sds((HOME, ROWS), BF16),
            sds((C, ROWS), BF16),
            sds((C, ROWS), BF16),
            sds((2 * C, ROWS), BF16),
            sds((512, ROWS), F32),
            sds((512, ROWS), F32),
            sds((512, ROWS), BF16),
            sds((C, ROWS), BF16),
            sds((C, ROWS), BF16),
            sds((8, ROWS), F32),
            sds((16, ROWS), F32),
            sds((C, 512), BF16),
        ],
        spot, recv, gain, entrance, portion, softness, base, exit_w,
        scalars=1,
    )
    token, saved = state[0], state[1:]
    token = swap(token, ("y", "core"))
    token = swap(spread_sum(token, GY, BF16), ("z", "x"))
    mix = call(
        token_kernel, sds((GX, MIX_ROWS, 128), BF16), token, request, lookup, content
    )
    mix = swap(mix, ("y", "core"))
    send, grads = call(
        backward_kernel,
        [sds((GY, SEND, C), BF16), sds((GY * GRAD_ROWS, 128), BF16)],
        mix, gain, entrance, softness, exit_w, *saved,
        scratch=[
            pltpu.VMEM((2 * C + 16, 512), BF16),
            pltpu.VMEM((2 * C + 16, ROWS), BF16),
            pltpu.VMEM((512, ROWS), F32),
            pltpu.VMEM((512, ROWS), BF16),
            pltpu.VMEM((2 * C, ROWS), BF16),
        ],
    )
    home = swap(send, ("z", "x"))
    grads = swap(grads.reshape(GY, GRAD_ROWS, 128), ("y", "core", "x"))
    grads = swap(spread_sum(grads, 8, BF16), ("z",))
    grads = swap(spread_sum(grads, GY, BF16), ("y", "core", "x"))
    result, cell_grad = call(
        unpack_kernel, [sds((SOUT * BLK, C), BF16), sds((SIN * BLK, C), BF16)], home
    )
    grad_in, grad_out, grad_slice = call(
        lambda *refs: weight_kernel(scale, *refs),
        [sds((C, 2 * C), F32), sds((C, C), F32), sds((WIDTH, SLICES), F32)],
        grads.reshape(GY * GRAD_ROWS, 128),
    )
    return result, cell_grad, grad_in, grad_out, grad_slice


def solution(mesh):
    grid = Mesh(mesh.devices.reshape(4, 2, 8, 4), ("y", "core", "z", "x"))
    whole = ("y", "core", "z", "x")
    placed = (P(whole, None), P(whole), P(whole, None), P(whole, None)) + (P(),) * 9
    return jax.shard_map(
        shards,
        mesh=grid,
        in_specs=placed,
        out_specs=(P(whole, None), P(whole, None), P(), P(), P()),
        check_vma=False,
    )
```

```python
import math

import jax
import jax.numpy as jnp
from jax import lax
from jax.experimental import pallas as pl
from jax.experimental.pallas import tpu as pltpu
from jax.sharding import Mesh, PartitionSpec as P

C = 256
HEADS = 8
SLICES = 64
WIDTH = 32
BLK = 128
SIN = 8
SOUT = 4
GX = 8
GY = 32
PIECE = BLK // GY
ROWS = GY * SOUT * PIECE
HOME = GY * SIN * PIECE
SEND = (SIN + SOUT) * PIECE
GROUP = 4 * SEND
META = 8
TALL = 2 * SEND + META
TOKEN_ROWS = 40
MIX_ROWS = 48
GRAD_ROWS = 56

norm_eps = 1e-05
slice_eps = 1e-05

F32 = jnp.float32
BF16 = jnp.bfloat16
HI = lax.Precision.HIGHEST
NN = (((1,), (0,)), ((), ()))
NT = (((1,), (1,)), ((), ()))
TN = (((0,), (0,)), ((), ()))


def mm(a, b, dims=NN, precision=None):
    return lax.dot_general(a, b, dims, precision=precision, preferred_element_type=F32)


def iota(shape, dim):
    return lax.broadcasted_iota(jnp.int32, shape, dim)


def call(body, outs, *args, scalars=0, scratch=(), flops=0, vmem=40):
    vm = pl.BlockSpec(memory_space=pltpu.VMEM)
    sm = pl.BlockSpec(memory_space=pltpu.SMEM)
    single = not isinstance(outs, (list, tuple))
    listed = [outs] if single else list(outs)
    moved = sum(math.prod(a.shape) * a.dtype.itemsize for a in list(args) + listed)
    res = pl.pallas_call(
        body,
        out_shape=listed,
        in_specs=[sm] * scalars + [vm] * (len(args) - scalars),
        out_specs=[vm] * len(listed),
        scratch_shapes=list(scratch),
        compiler_params=pltpu.CompilerParams(vmem_limit_bytes=vmem * 2**20),
        cost_estimate=pl.CostEstimate(flops=flops, bytes_accessed=moved, transcendentals=0),
    )(*args)
    return res[0] if single else res


def sds(shape, dtype):
    return jax.ShapeDtypeStruct(shape, dtype)


def column(row):
    n = row.shape[1]
    return jnp.sum(jnp.where(iota((n, n), 0) == iota((n, n), 1), row, 0.0), axis=1, keepdims=True)


def piece_order(back):
    sent = iota((GROUP, GROUP), 1 if back else 0)
    kept = iota((GROUP, GROUP), 0 if back else 1)
    part = (
        (sent >= SEND).astype(jnp.int32)
        + (sent >= 2 * SEND).astype(jnp.int32)
        + (sent >= 3 * SEND).astype(jnp.int32)
    )
    within = sent - part * SEND
    source = (within >> 2) * 16 + part * PIECE + (within & 3)
    return (source == kept).astype(F32).astype(BF16)


def pack_kernel(tally, plan, cells, cot, out):
    order = piece_order(False)
    for j in range(8):
        at = 16 * j
        rows = [cells[s * BLK + at : s * BLK + at + 16, :] for s in range(SIN)]
        rows += [cot[t * BLK + at : t * BLK + at + 16, :] for t in range(SOUT)]
        moved = mm(order, jnp.concatenate(rows, axis=0)).astype(BF16)
        for a in range(4):
            part = moved[a * SEND : (a + 1) * SEND]
            out[4 * j + a, 0:SEND, :] = part[:, 0:128]
            out[4 * j + a, SEND : 2 * SEND, :] = part[:, 128:C]
    block = iota((META, 128), 1) >> 2
    target = jnp.zeros((META, 128), jnp.int32)
    for s in range(SIN):
        target = jnp.where(block == s, plan[0, s], target)
    held = jnp.clip(tally[0] - block * BLK, 0, BLK)
    meta = jnp.where(iota((META, 128), 0) < 4, target, held).astype(F32).astype(BF16)
    for j in range(GY):
        out[j, 2 * SEND : TALL, :] = meta


def unpack_kernel(recv, result, cell_grad):
    order = piece_order(True)
    for j in range(8):
        at = 16 * j
        rows = jnp.concatenate([recv[4 * j + a] for a in range(4)], axis=0)
        moved = mm(order, rows).astype(BF16)
        for s in range(SIN):
            cell_grad[s * BLK + at : s * BLK + at + 16, :] = moved[s * 16 : s * 16 + 16]
        for t in range(SOUT):
            u = SIN + t
            result[t * BLK + at : t * BLK + at + 16, :] = moved[u * 16 : u * 16 + 16]


def forward_kernel(
    spot, recv, gain, entrance, portion, softness, base, exit_w,
    token, pick, xt_out, normed_out, proj_out, prob_out, scaled_out, slice_out,
    uns_out, cot_out, rows_out, heads_out, spread_out,
):
    mine = spot[0]
    cells = jnp.concatenate(
        [recv[:, a : a + SIN * PIECE, :].reshape(HOME, 128) for a in (0, SEND)], axis=1
    )
    cot = jnp.concatenate(
        [recv[:, a + SIN * PIECE : a + SEND, :].reshape(ROWS, 128) for a in (0, SEND)], axis=1
    )
    meta = recv[:, 2 * SEND : TALL, :].astype(F32)
    upper = iota((GY, META, 128), 1) < 4
    target = jnp.max(jnp.where(upper, meta, -1.0), axis=1)
    held = jnp.max(jnp.where(upper, 0.0, meta), axis=1)

    lane = iota((GY, 128), 1)
    lane_f = lane.astype(F32)
    hits = [(target[:, 4 * s : 4 * s + 1] == lane_f).astype(F32) for s in range(SIN)]
    taken = hits[0]
    for s in range(1, SIN):
        taken = taken + hits[s]
    before = (iota((GY, GY), 1) < iota((GY, GY), 0)).astype(F32).astype(BF16)
    place = mm(before, taken.astype(BF16)) + lane_f * SOUT + 1.0
    dest = jnp.zeros((GY, 128), F32)
    for s in range(SIN):
        found = jnp.sum(hits[s] * place, axis=1, keepdims=True)
        dest = jnp.where((lane >> 2) == s, found, dest)
    row_in_block = (mine * PIECE + (lane & 3)).astype(F32)
    dest = jnp.where(row_in_block < held, dest, 0.0) - 1.0
    repeat = ((iota((HOME, GY), 0) >> 5) == iota((HOME, GY), 1)).astype(F32).astype(BF16)
    wide = mm(repeat, dest.astype(BF16))
    own = iota((HOME, 128), 1) == (iota((HOME, 128), 0) & 31)
    dest_col = jnp.sum(jnp.where(own, wide, 0.0), axis=1, keepdims=True)
    k_col = (iota((HOME, 1), 0) & 3).astype(F32)
    spot_col = (dest_col * 4.0 + k_col).astype(jnp.int32)
    pick[...] = (spot_col == iota((HOME, ROWS), 1)).astype(F32).astype(BF16)
    live = mm(jnp.ones((8, HOME), BF16), pick[...])[0:1, :]

    xt = mm(cells, pick[...], TN)
    xt_out[...] = xt.astype(BF16)
    mean = jnp.sum(xt, axis=0, keepdims=True) * (1.0 / C)
    centered = xt - mean
    var = jnp.sum(centered * centered, axis=0, keepdims=True) * (1.0 / C)
    inv = lax.rsqrt(var + norm_eps)
    gain_col = column(gain[...])
    normed = (centered * inv * gain_col).astype(BF16)
    normed_out[...] = normed
    proj_out[...] = mm(entrance[...], normed, TN).astype(BF16)
    rows_out[0:1, :] = live
    rows_out[1:2, :] = mean
    rows_out[2:3, :] = inv

    tall = ((iota((C, WIDTH), 0) & 31) == iota((C, WIDTH), 1)).astype(F32).astype(BF16)
    broad = ((iota((SLICES, 512), 1) & 63) == iota((SLICES, 512), 0)).astype(F32).astype(BF16)
    spread = mm(mm(tall, portion[...]).astype(BF16), broad)
    same = (iota((C, 512), 0) >> 5) == (iota((C, 512), 1) >> 6)
    spread_out[...] = jnp.where(same, spread, 0.0).astype(BF16)
    soft_row = mm(softness[...], tall, NT)
    soft_same = (iota((HEADS, C), 1) >> 5) == iota((HEADS, C), 0)
    soft_spread = jnp.where(soft_same, soft_row, 0.0).astype(BF16)

    mid = proj_out[C : 2 * C, :]
    presq = mm(soft_spread, mid)
    softplus = jnp.maximum(presq, 0.0) + jnp.log1p(jnp.exp(-jnp.abs(presq)))
    inv_temp = 1.0 / (column(base[...]) + softplus)
    heads_out[0:8, :] = inv_temp
    heads_out[8:16, :] = presq
    scaled_out[...] = mm(spread_out[...], mid, TN)

    back = mm(exit_w[...], cot, NT) * live
    uns_out[...] = back.astype(BF16)
    eye = (iota((C, C), 0) == iota((C, C), 1)).astype(F32).astype(BF16)
    cot_out[...] = (mm(eye, cot, NT) * live).astype(BF16)

    for h in range(HEADS):
        at = h * SLICES
        scaled = scaled_out[at : at + SLICES, :] * inv_temp[h : h + 1, :]
        scaled_out[at : at + SLICES, :] = scaled
        top = jnp.max(scaled, axis=0, keepdims=True)
        e = jnp.exp(scaled - top)
        prob = e * (1.0 / jnp.sum(e, axis=0, keepdims=True))
        prob_out[at : at + SLICES, :] = prob
        half = (prob * live).astype(BF16)
        slice_out[at : at + SLICES, :] = half
        left = jnp.concatenate(
            [
                proj_out[h * WIDTH : (h + 1) * WIDTH, :],
                uns_out[h * WIDTH : (h + 1) * WIDTH, :],
                jnp.ones((16, ROWS), BF16),
            ],
            axis=0,
        )
        sums = mm(left, half, NT)
        main = jnp.concatenate([sums[0:WIDTH], sums[WIDTH : 2 * WIDTH]], axis=1)
        count = jnp.concatenate([sums[2 * WIDTH : 2 * WIDTH + 8]] * 2, axis=1)
        token[h] = jnp.concatenate([main, count], axis=0).astype(BF16)


def spread_kernel(recv, out):
    n = recv.shape[0]
    total = recv[0].astype(F32)
    for i in range(1, n):
        total = total + recv[i].astype(F32)
    total = total.astype(out.dtype)
    for i in range(out.shape[0]):
        out[i] = total


def spread_sum(recv, copies, dtype):
    return call(spread_kernel, sds((copies,) + recv.shape[1:], dtype), recv)


def token_kernel(recv, request, lookup, content, out):
    total = recv[0].astype(F32)
    for i in range(1, GY):
        total = total + recv[i].astype(F32)
    inverse = 1.0 / (total[WIDTH : WIDTH + 1, 0:SLICES] + slice_eps)
    tok = total[0:WIDTH, 0:SLICES] * inverse
    cot = total[0:WIDTH, SLICES:128]
    scale = WIDTH ** (-0.5)
    q = mm(request[...], tok, TN, HI)
    k = mm(lookup[...], tok, TN, HI)
    v = mm(content[...], tok, TN, HI)
    scores = mm(k, q, TN, HI) * scale
    e = jnp.exp(scores - jnp.max(scores, axis=0, keepdims=True))
    att = e / jnp.sum(e, axis=0, keepdims=True)
    mixed = mm(v, att, NN, HI)
    g_att = mm(v, cot, TN, HI)
    g_v = mm(cot, att, NT, HI)
    g_s = att * (g_att - jnp.sum(att * g_att, axis=0, keepdims=True)) * scale
    g_q = mm(k, g_s, NN, HI)
    g_k = mm(q, g_s, NT, HI)
    g_tok = mm(request[...], g_q, NN, HI)
    g_tok = g_tok + mm(lookup[...], g_k, NN, HI)
    g_tok = g_tok + mm(content[...], g_v, NN, HI)
    g_num = g_tok * inverse
    g_den = -jnp.sum(g_tok * tok, axis=0, keepdims=True) * inverse
    g_den_hi = g_den.astype(BF16).astype(F32)
    g_den_lo = g_den - g_den_hi
    main = jnp.concatenate([mixed, g_num], axis=1).astype(BF16)
    tail = jnp.concatenate([g_den_hi, g_den_lo], axis=1)
    tail = jnp.broadcast_to(tail, (16, 128)).astype(BF16)
    for i in range(GX):
        out[i, 0:WIDTH, :] = main
        out[i, WIDTH:MIX_ROWS, :] = tail


def backward_kernel(
    mix, gain, entrance, softness, exit_w,
    pick, xt_in, normed_in, proj_in, prob_in, scaled_in, slice_in,
    uns_in, cot_in, rows_in, heads_in, spread_in,
    send, grads, weave, stack, gprob, affs, gproj,
):
    live = rows_in[0:1, :]
    mean = rows_in[1:2, :]
    inv = rows_in[2:3, :]
    weave[...] = jnp.zeros_like(weave)
    lane = iota((WIDTH, 128), 1)
    lane16 = iota((16, 128), 1)
    sub16 = iota((16, 128), 0)
    for h in range(HEADS):
        block = mix[h].astype(F32)
        turned = pltpu.roll(block, SLICES, 1)
        low = h % 2 == 0
        left, right = (block, turned) if low else (turned, block)
        here = (lane < SLICES) if low else (lane >= SLICES)
        at = (h // 2) * 128
        weave[h * WIDTH : (h + 1) * WIDTH, at : at + 128] = jnp.where(
            here, left[0:WIDTH], 0.0
        ).astype(BF16)
        weave[C + h * WIDTH : C + (h + 1) * WIDTH, at : at + 128] = jnp.where(
            here, right[0:WIDTH], 0.0
        ).astype(BF16)
    for g in range(HEADS // 2):
        even = mix[2 * g, WIDTH:MIX_ROWS, :].astype(F32)
        odd = mix[2 * g + 1, WIDTH:MIX_ROWS, :].astype(F32)
        upper = jnp.where(lane16 < SLICES, even, pltpu.roll(odd, SLICES, 1))
        lower = jnp.where(lane16 < SLICES, pltpu.roll(even, SLICES, 1), odd)
        both = jnp.where(sub16 == 0, upper, jnp.where(sub16 == 1, lower, 0.0))
        weave[2 * C : 2 * C + 16, g * 128 : (g + 1) * 128] = both.astype(BF16)
    stack[0:C, :] = uns_in[...]
    stack[C : 2 * C, :] = proj_in[0:C, :]
    stack[2 * C : 2 * C + 16, :] = jnp.ones((16, ROWS), BF16)

    rows = mm(weave[0 : 2 * C, :], slice_in[...])
    deslice = rows[0:C].astype(BF16)
    gproj[0:C, :] = rows[C : 2 * C].astype(BF16)
    gprob[...] = mm(weave[...], stack[...], TN)
    branch = mm(exit_w[...], deslice, TN)
    xt = xt_in[...].astype(F32)
    result = (live * (xt + branch)).astype(BF16)
    eye = (iota((ROWS, ROWS), 0) == iota((ROWS, ROWS), 1)).astype(F32).astype(BF16)
    result_rows = mm(eye, result, NT).astype(BF16)
    for q in range(GY):
        send[q, SIN * PIECE : SEND, :] = result_rows[q * 16 : (q + 1) * 16]
    out_grad = mm(deslice, cot_in[...], NT)
    for b in range(2):
        grads[(4 + b) * C : (5 + b) * C, :] = out_grad[:, b * 128 : (b + 1) * 128].astype(
            grads.dtype
        )

    softs = []
    for h in range(HEADS):
        at = h * SLICES
        inv_temp = heads_in[h : h + 1, :]
        presq = heads_in[8 + h : 9 + h, :]
        prob = prob_in[at : at + SLICES, :]
        gp = gprob[at : at + SLICES, :] * live
        adj = prob * (gp - jnp.sum(prob * gp, axis=0, keepdims=True))
        affs[at : at + SLICES, :] = (adj * inv_temp).astype(BF16)
        pulled = jnp.sum(adj * scaled_in[at : at + SLICES, :], axis=0, keepdims=True)
        softs.append(-pulled * inv_temp * (1.0 / (1.0 + jnp.exp(-presq))))
    between = mm(spread_in[...], affs[...])
    soft_col = column(softness[...].astype(F32))
    slice_grad = jnp.zeros((WIDTH, SLICES), F32)
    for h in range(HEADS):
        at = h * WIDTH
        part = between[at : at + WIDTH] + soft_col * softs[h]
        gproj[C + at : C + at + WIDTH, :] = part.astype(BF16)
        slice_grad = slice_grad + mm(
            proj_in[C + at : C + at + WIDTH, :], affs[h * SLICES : (h + 1) * SLICES, :], NT
        )
    in_grad = mm(normed_in[...], gproj[...], NT)
    for b in range(4):
        grads[b * C : (b + 1) * C, :] = in_grad[:, b * 128 : (b + 1) * 128].astype(grads.dtype)
    tail = jnp.concatenate([slice_grad, jnp.zeros((WIDTH, SLICES), F32)], axis=1)
    grads[6 * C : 6 * C + WIDTH, :] = tail.astype(grads.dtype)
    grads[6 * C + WIDTH :, :] = jnp.zeros((GY * GRAD_ROWS - 6 * C - WIDTH, 128), grads.dtype)

    g_unit = mm(entrance[...], gproj[...]) * column(gain[...])
    unit = (xt - mean) * inv
    m1 = jnp.sum(g_unit, axis=0, keepdims=True) * (1.0 / C)
    m2 = jnp.sum(g_unit * unit, axis=0, keepdims=True) * (1.0 / C)
    cell = cot_in[...].astype(F32) + inv * (g_unit - m1 - unit * m2)
    cell_rows = mm(pick[...], cell.astype(BF16), NT).astype(BF16)
    for q in range(GY):
        send[q, 0 : SIN * PIECE, :] = cell_rows[q * 32 : (q + 1) * 32]


def weight_kernel(scale, at, r0, r1, r2, r3, grad_in, grad_out, grad_slice, flat):
    y, core, x = at[0], at[1], at[2]
    for dy, recv in enumerate((r0, r1, r2, r3)):
        for dx in range(4):
            for dc in range(2):
                index = (((y - dy) & 3) * 2 + (core ^ dc)) * 4 + ((x - dx) & 3)
                start = pl.multiple_of(index * GRAD_ROWS, 8)
                flat[pl.ds(start, GRAD_ROWS), :] = recv[dx * 2 + dc].astype(F32) * scale

    def part(b):
        return flat[b * C : (b + 1) * C, :]

    for b in range(4):
        grad_in[:, b * 128 : (b + 1) * 128] = part(b)
    for b in range(2):
        grad_out[:, b * 128 : (b + 1) * 128] = part(4 + b)
    grad_slice[...] = flat[6 * C : 6 * C + WIDTH, 0:SLICES]


def shards(
    cells, tally, plan, cot, gain, entrance, portion, softness, base,
    request, lookup, content, exit_w,
):
    gain = gain.reshape(1, C)
    softness = softness.reshape(1, WIDTH)
    base = base.reshape(1, HEADS)
    scale = 1.0 / math.sqrt(GX * GY * SIN * BLK)

    def swap(x, axes):
        return lax.all_to_all(x, axes, 0, 0, tiled=True)

    def shifted(x, axis, n, d):
        return lax.ppermute(x, axis, [(i, (i + d) % n) for i in range(n)])

    sent = call(
        pack_kernel, sds((GY, TALL, 128), BF16), tally, plan, cells, cot, scalars=2
    )
    recv = swap(sent, ("z", "x"))
    spot = (lax.axis_index("z") * 4 + lax.axis_index("x")).astype(jnp.int32).reshape(1)
    state = call(
        forward_kernel,
        [
            sds((HEADS, TOKEN_ROWS, 128), BF16),
            sds((HOME, ROWS), BF16),
            sds((C, ROWS), BF16),
            sds((C, ROWS), BF16),
            sds((2 * C, ROWS), BF16),
            sds((512, ROWS), F32),
            sds((512, ROWS), F32),
            sds((512, ROWS), BF16),
            sds((C, ROWS), BF16),
            sds((C, ROWS), BF16),
            sds((8, ROWS), F32),
            sds((16, ROWS), F32),
            sds((C, 512), BF16),
        ],
        spot, recv, gain, entrance, portion, softness, base, exit_w,
        scalars=1,
    )
    token, saved = state[0], state[1:]
    token = swap(token, ("y", "core"))
    token = swap(spread_sum(token, GY, BF16), ("z", "x"))
    mix = call(
        token_kernel, sds((GX, MIX_ROWS, 128), BF16), token, request, lookup, content
    )
    mix = swap(mix, ("y", "core"))
    send, grads = call(
        backward_kernel,
        [sds((GY, SEND, C), BF16), sds((GY * GRAD_ROWS, 128), BF16)],
        mix, gain, entrance, softness, exit_w, *saved,
        scratch=[
            pltpu.VMEM((2 * C + 16, 512), BF16),
            pltpu.VMEM((2 * C + 16, ROWS), BF16),
            pltpu.VMEM((512, ROWS), F32),
            pltpu.VMEM((512, ROWS), BF16),
            pltpu.VMEM((2 * C, ROWS), BF16),
        ],
    )
    grads = swap(grads.reshape(GY, GRAD_ROWS, 128), ("y", "core", "x"))
    grads = swap(spread_sum(grads, 8, BF16), ("z",))
    grads = spread_sum(grads, 1, BF16)
    send, grads = lax.optimization_barrier((send, grads))
    home = swap(send, ("z", "x"))
    grads = jnp.concatenate([grads, shifted(grads, "core", 2, 1)], axis=0)
    grads = jnp.concatenate([grads] + [shifted(grads, "x", 4, d) for d in (1, 2, 3)], axis=0)
    gathered = [grads] + [shifted(grads, "y", 4, d) for d in (1, 2, 3)]
    at = jnp.stack([lax.axis_index(a) for a in ("y", "core", "x")]).astype(jnp.int32)
    result, cell_grad = call(
        unpack_kernel, [sds((SOUT * BLK, C), BF16), sds((SIN * BLK, C), BF16)], home
    )
    grad_in, grad_out, grad_slice = call(
        lambda *refs: weight_kernel(scale, *refs),
        [sds((C, 2 * C), F32), sds((C, C), F32), sds((WIDTH, SLICES), F32)],
        at, *gathered,
        scalars=1,
        scratch=[pltpu.VMEM((GY * GRAD_ROWS, 128), F32)],
    )
    return result, cell_grad, grad_in, grad_out, grad_slice


def solution(mesh):
    grid = Mesh(mesh.devices.reshape(4, 2, 8, 4), ("y", "core", "z", "x"))
    whole = ("y", "core", "z", "x")
    placed = (P(whole, None), P(whole), P(whole, None), P(whole, None)) + (P(),) * 9
    return jax.shard_map(
        shards,
        mesh=grid,
        in_specs=placed,
        out_specs=(P(whole, None), P(whole, None), P(), P(), P()),
        check_vma=False,
    )
```

```python
import math

import jax
import jax.numpy as jnp
from jax import lax
from jax.experimental import pallas as pl
from jax.experimental.pallas import tpu as pltpu
from jax.sharding import Mesh, PartitionSpec as P

C = 256
HEADS = 8
SLICES = 64
WIDTH = 32
BLK = 128
SIN = 8
SOUT = 4
GX = 8
GY = 32
PIECE = BLK // GY
ROWS = GY * SOUT * PIECE
HOME = GY * SIN * PIECE
SEND = (SIN + SOUT) * PIECE
GROUP = 4 * SEND
META = 8
TALL = 2 * SEND + META
TOKEN_ROWS = 40
MIX_ROWS = 48
GRAD_ROWS = 56

norm_eps = 1e-05
slice_eps = 1e-05

F32 = jnp.float32
BF16 = jnp.bfloat16
HI = lax.Precision.HIGHEST
NN = (((1,), (0,)), ((), ()))
NT = (((1,), (1,)), ((), ()))
TN = (((0,), (0,)), ((), ()))


def mm(a, b, dims=NN, precision=None):
    return lax.dot_general(a, b, dims, precision=precision, preferred_element_type=F32)


def iota(shape, dim):
    return lax.broadcasted_iota(jnp.int32, shape, dim)


def call(body, outs, *args, scalars=0, hbm=False, hbm_out=False, scratch=(), vmem=40):
    vm = pl.BlockSpec(memory_space=pltpu.VMEM)
    sm = pl.BlockSpec(memory_space=pltpu.SMEM)
    far = pl.BlockSpec(memory_space=pltpu.HBM)
    single = not isinstance(outs, (list, tuple))
    listed = [outs] if single else list(outs)
    moved = sum(math.prod(a.shape) * a.dtype.itemsize for a in list(args) + listed)
    res = pl.pallas_call(
        body,
        out_shape=listed,
        in_specs=[sm] * scalars + [far if hbm else vm] * (len(args) - scalars),
        out_specs=[far if hbm_out else vm] * len(listed),
        scratch_shapes=list(scratch),
        compiler_params=pltpu.CompilerParams(vmem_limit_bytes=vmem * 2**20),
        cost_estimate=pl.CostEstimate(flops=0, bytes_accessed=moved, transcendentals=0),
    )(*args)
    return res[0] if single else res


def sds(shape, dtype):
    return jax.ShapeDtypeStruct(shape, dtype)


def column(row):
    n = row.shape[1]
    return jnp.sum(jnp.where(iota((n, n), 0) == iota((n, n), 1), row, 0.0), axis=1, keepdims=True)


def piece_order(back):
    sent = iota((GROUP, GROUP), 1 if back else 0)
    kept = iota((GROUP, GROUP), 0 if back else 1)
    part = (
        (sent >= SEND).astype(jnp.int32)
        + (sent >= 2 * SEND).astype(jnp.int32)
        + (sent >= 3 * SEND).astype(jnp.int32)
    )
    within = sent - part * SEND
    source = (within >> 2) * 16 + part * PIECE + (within & 3)
    return (source == kept).astype(F32).astype(BF16)


def pack_kernel(tally_hbm, plan_hbm, cells, cot, out, tally, plan, rows, sent, small_sem, in_sem, out_sem):
    small = [
        pltpu.make_async_copy(tally_hbm, tally, small_sem.at[0]),
        pltpu.make_async_copy(plan_hbm, plan, small_sem.at[1]),
    ]
    for copy in small:
        copy.start()
    reads = []
    for j in range(8):
        at = pl.ds(16 * j, 16)
        pair = [
            pltpu.make_async_copy(cells.at[:, at, :], rows.at[j, 0:SIN], in_sem.at[j, 0]),
            pltpu.make_async_copy(cot.at[:, at, :], rows.at[j, SIN : SIN + SOUT], in_sem.at[j, 1]),
        ]
        for copy in pair:
            copy.start()
        reads.append(pair)
    order = piece_order(False)
    for copy in small:
        copy.wait()
    block = iota((META, 128), 1) >> 2
    target = jnp.zeros((META, 128), jnp.int32)
    for s in range(SIN):
        target = jnp.where(block == s, plan[0, s], target)
    held = jnp.clip(tally[0] - block * BLK, 0, BLK)
    meta = jnp.where(iota((META, 128), 0) < 4, target, held).astype(F32).astype(BF16)
    for j in range(GY):
        sent[j, 2 * SEND : TALL, :] = meta
    writes = []
    for j in range(8):
        for copy in reads[j]:
            copy.wait()
        moved = mm(order, rows[j].reshape(GROUP, C)).astype(BF16)
        for a in range(4):
            part = moved[a * SEND : (a + 1) * SEND]
            sent[4 * j + a, 0:SEND, :] = part[:, 0:128]
            sent[4 * j + a, SEND : 2 * SEND, :] = part[:, 128:C]
        group = pl.ds(4 * j, 4)
        copy = pltpu.make_async_copy(sent.at[group], out.at[group], out_sem.at[j])
        copy.start()
        writes.append(copy)
    for copy in writes:
        copy.wait()


def weight_kernel(
    gain, entrance, portion, softness, base, exit_w,
    entrance_t, exit_t, spread_out, soft_spread_out, gain_out, base_out, soft_out,
):
    eye = (iota((C, C), 0) == iota((C, C), 1)).astype(F32).astype(BF16)
    entrance_t[...] = mm(entrance[...], eye, TN).astype(BF16)
    exit_t[...] = mm(exit_w[...], eye, TN).astype(BF16)
    tall = ((iota((C, WIDTH), 0) & 31) == iota((C, WIDTH), 1)).astype(F32).astype(BF16)
    broad = ((iota((SLICES, 512), 1) & 63) == iota((SLICES, 512), 0)).astype(F32).astype(BF16)
    spread = mm(mm(tall, portion[...]).astype(BF16), broad)
    same = (iota((C, 512), 0) >> 5) == (iota((C, 512), 1) >> 6)
    spread_out[...] = jnp.where(same, spread, 0.0).astype(BF16)
    soft_row = mm(softness[...], tall, NT)
    soft_same = (iota((16, C), 1) >> 5) == iota((16, C), 0)
    soft_spread_out[...] = jnp.where(soft_same, soft_row, 0.0).astype(BF16)
    gain_out[...] = jnp.broadcast_to(column(gain[...]), (C, 128))
    base_out[...] = jnp.broadcast_to(column(base[...]), (HEADS, 128))
    soft_out[...] = jnp.broadcast_to(column(softness[...].astype(F32)), (WIDTH, 128))


def forward_kernel(
    spot, recv, entrance_t, exit_w, spread, soft_spread, gain_col, base_col,
    token, pick, xt_out, normed_out, proj_out, prob_out, scaled_out, slice_out,
    uns_out, cot_out, rows_out, heads_out,
):
    mine = spot[0]
    cells = jnp.concatenate(
        [recv[:, a : a + SIN * PIECE, :].reshape(HOME, 128) for a in (0, SEND)], axis=1
    )
    cot = jnp.concatenate(
        [recv[:, a + SIN * PIECE : a + SEND, :].reshape(ROWS, 128) for a in (0, SEND)], axis=1
    )
    meta = recv[:, 2 * SEND : TALL, :].astype(F32)
    upper = iota((GY, META, 128), 1) < 4
    target = jnp.max(jnp.where(upper, meta, -1.0), axis=1)
    held = jnp.max(jnp.where(upper, 0.0, meta), axis=1)

    lane = iota((GY, 128), 1)
    lane_f = lane.astype(F32)
    hits = [(target[:, 4 * s : 4 * s + 1] == lane_f).astype(F32) for s in range(SIN)]
    taken = hits[0]
    for s in range(1, SIN):
        taken = taken + hits[s]
    before = (iota((GY, GY), 1) < iota((GY, GY), 0)).astype(F32).astype(BF16)
    place = mm(before, taken.astype(BF16)) + lane_f * SOUT + 1.0
    dest = jnp.zeros((GY, 128), F32)
    for s in range(SIN):
        found = jnp.sum(hits[s] * place, axis=1, keepdims=True)
        dest = jnp.where((lane >> 2) == s, found, dest)
    row_in_block = (mine * PIECE + (lane & 3)).astype(F32)
    dest = jnp.where(row_in_block < held, dest, 0.0) - 1.0
    flip = (iota((128, 128), 0) == iota((128, 128), 1)).astype(F32).astype(BF16)
    slots = mm(flip, dest.astype(BF16), NT)[0:32, :]
    slots = (slots * 4.0 + (iota((32, GY), 0) & 3).astype(F32)).astype(jnp.int32)
    at_row = iota((32, ROWS), 1)
    seen = jnp.zeros((32, ROWS), F32)
    for p in range(GY):
        match = (slots[:, p : p + 1] == at_row).astype(F32)
        seen = seen + match
        pick[p * 32 : (p + 1) * 32, :] = match.astype(BF16)
    live = jnp.sum(seen, axis=0, keepdims=True)

    xt = mm(cells, pick[...], TN)
    xt_out[...] = xt.astype(BF16)
    mean = jnp.sum(xt, axis=0, keepdims=True) * (1.0 / C)
    centered = xt - mean
    var = jnp.sum(centered * centered, axis=0, keepdims=True) * (1.0 / C)
    inv = lax.rsqrt(var + norm_eps)
    normed = (centered * inv * gain_col[:, 0:1]).astype(BF16)
    normed_out[...] = normed
    proj_out[...] = mm(entrance_t[...], normed).astype(BF16)
    rows_out[0:1, :] = live
    rows_out[1:2, :] = mean
    rows_out[2:3, :] = inv

    mid = proj_out[C : 2 * C, :]
    presq = mm(soft_spread[...], mid)[0:HEADS]
    softplus = jnp.maximum(presq, 0.0) + jnp.log1p(jnp.exp(-jnp.abs(presq)))
    inv_temp = 1.0 / (base_col[:, 0:1] + softplus)
    heads_out[0:8, :] = inv_temp
    heads_out[8:16, :] = presq
    scaled_out[...] = mm(spread[...], mid, TN)

    back = mm(exit_w[...], cot, NT) * live
    uns_out[...] = back.astype(BF16)
    eye = (iota((C, C), 0) == iota((C, C), 1)).astype(F32).astype(BF16)
    cot_out[...] = (mm(eye, cot, NT) * live).astype(BF16)

    for h in range(HEADS):
        at = h * SLICES
        scaled = scaled_out[at : at + SLICES, :] * inv_temp[h : h + 1, :]
        scaled_out[at : at + SLICES, :] = scaled
        top = jnp.max(scaled, axis=0, keepdims=True)
        e = jnp.exp(scaled - top)
        prob = e * (1.0 / jnp.sum(e, axis=0, keepdims=True))
        prob_out[at : at + SLICES, :] = prob
        half = (prob * live).astype(BF16)
        slice_out[at : at + SLICES, :] = half
        left = jnp.concatenate(
            [
                proj_out[h * WIDTH : (h + 1) * WIDTH, :],
                uns_out[h * WIDTH : (h + 1) * WIDTH, :],
                jnp.ones((16, ROWS), BF16),
            ],
            axis=0,
        )
        sums = mm(left, half, NT)
        main = jnp.concatenate([sums[0:WIDTH], sums[WIDTH : 2 * WIDTH]], axis=1)
        count = jnp.concatenate([sums[2 * WIDTH : 2 * WIDTH + 8]] * 2, axis=1)
        token[h] = jnp.concatenate([main, count], axis=0).astype(BF16)


def spread_kernel(recv, out):
    n = recv.shape[0]
    total = recv[0].astype(F32)
    for i in range(1, n):
        total = total + recv[i].astype(F32)
    total = total.astype(out.dtype)
    for i in range(out.shape[0]):
        out[i] = total


def spread_sum(recv, copies, dtype):
    return call(spread_kernel, sds((copies,) + recv.shape[1:], dtype), recv)


def token_kernel(recv, request, lookup, content, out):
    total = recv[0].astype(F32)
    for i in range(1, GY):
        total = total + recv[i].astype(F32)
    inverse = 1.0 / (total[WIDTH : WIDTH + 1, 0:SLICES] + slice_eps)
    tok = total[0:WIDTH, 0:SLICES] * inverse
    cot = total[0:WIDTH, SLICES:128]
    scale = WIDTH ** (-0.5)
    q = mm(request[...], tok, TN, HI)
    k = mm(lookup[...], tok, TN, HI)
    v = mm(content[...], tok, TN, HI)
    scores = mm(k, q, TN, HI) * scale
    e = jnp.exp(scores - jnp.max(scores, axis=0, keepdims=True))
    att = e / jnp.sum(e, axis=0, keepdims=True)
    mixed = mm(v, att, NN, HI)
    g_att = mm(v, cot, TN, HI)
    g_v = mm(cot, att, NT, HI)
    g_s = att * (g_att - jnp.sum(att * g_att, axis=0, keepdims=True)) * scale
    g_q = mm(k, g_s, NN, HI)
    g_k = mm(q, g_s, NT, HI)
    g_tok = mm(request[...], g_q, NN, HI)
    g_tok = g_tok + mm(lookup[...], g_k, NN, HI)
    g_tok = g_tok + mm(content[...], g_v, NN, HI)
    g_num = g_tok * inverse
    g_den = -jnp.sum(g_tok * tok, axis=0, keepdims=True) * inverse
    g_den_hi = g_den.astype(BF16).astype(F32)
    g_den_lo = g_den - g_den_hi
    main = jnp.concatenate([mixed, g_num], axis=1).astype(BF16)
    tail = jnp.concatenate([g_den_hi, g_den_lo], axis=1)
    tail = jnp.broadcast_to(tail, (16, 128)).astype(BF16)
    for i in range(GX):
        out[i, 0:WIDTH, :] = main
        out[i, WIDTH:MIX_ROWS, :] = tail


def backward_kernel(
    mix, entrance, exit_t, spread, gain_col, soft_col,
    pick, xt_in, normed_in, proj_in, prob_in, scaled_in, slice_in,
    uns_in, cot_in, rows_in, heads_in,
    send, grads, weave, stack, gprob, affs, gproj,
):
    live = rows_in[0:1, :]
    mean = rows_in[1:2, :]
    inv = rows_in[2:3, :]
    weave[...] = jnp.zeros_like(weave)
    lane = iota((WIDTH, 128), 1)
    lane16 = iota((16, 128), 1)
    sub16 = iota((16, 128), 0)
    for h in range(HEADS):
        block = mix[h].astype(F32)
        turned = pltpu.roll(block, SLICES, 1)
        low = h % 2 == 0
        left, right = (block, turned) if low else (turned, block)
        here = (lane < SLICES) if low else (lane >= SLICES)
        at = (h // 2) * 128
        weave[h * WIDTH : (h + 1) * WIDTH, at : at + 128] = jnp.where(
            here, left[0:WIDTH], 0.0
        ).astype(BF16)
        weave[C + h * WIDTH : C + (h + 1) * WIDTH, at : at + 128] = jnp.where(
            here, right[0:WIDTH], 0.0
        ).astype(BF16)
    for g in range(HEADS // 2):
        even = mix[2 * g, WIDTH:MIX_ROWS, :].astype(F32)
        odd = mix[2 * g + 1, WIDTH:MIX_ROWS, :].astype(F32)
        upper = jnp.where(lane16 < SLICES, even, pltpu.roll(odd, SLICES, 1))
        lower = jnp.where(lane16 < SLICES, pltpu.roll(even, SLICES, 1), odd)
        both = jnp.where(sub16 == 0, upper, jnp.where(sub16 == 1, lower, 0.0))
        weave[2 * C : 2 * C + 16, g * 128 : (g + 1) * 128] = both.astype(BF16)
    stack[0:C, :] = uns_in[...]
    stack[C : 2 * C, :] = proj_in[0:C, :]
    stack[2 * C : 2 * C + 16, :] = jnp.ones((16, ROWS), BF16)

    rows = mm(weave[0 : 2 * C, :], slice_in[...])
    deslice = rows[0:C].astype(BF16)
    gproj[0:C, :] = rows[C : 2 * C].astype(BF16)
    gprob[...] = mm(weave[...], stack[...], TN)
    branch = mm(exit_t[...], deslice)
    xt = xt_in[...].astype(F32)
    result = (live * (xt + branch)).astype(BF16)
    eye = (iota((ROWS, ROWS), 0) == iota((ROWS, ROWS), 1)).astype(F32).astype(BF16)
    result_rows = mm(eye, result, NT).astype(BF16)
    for q in range(GY):
        send[q, SIN * PIECE : SEND, :] = result_rows[q * 16 : (q + 1) * 16]
    out_grad = mm(deslice, cot_in[...], NT)
    for b in range(2):
        grads[(4 + b) * C : (5 + b) * C, :] = out_grad[:, b * 128 : (b + 1) * 128].astype(
            grads.dtype
        )

    softs = []
    for h in range(HEADS):
        at = h * SLICES
        inv_temp = heads_in[h : h + 1, :]
        presq = heads_in[8 + h : 9 + h, :]
        prob = prob_in[at : at + SLICES, :]
        gp = gprob[at : at + SLICES, :] * live
        adj = prob * (gp - jnp.sum(prob * gp, axis=0, keepdims=True))
        affs[at : at + SLICES, :] = (adj * inv_temp).astype(BF16)
        pulled = jnp.sum(adj * scaled_in[at : at + SLICES, :], axis=0, keepdims=True)
        softs.append(-pulled * inv_temp * (1.0 / (1.0 + jnp.exp(-presq))))
    between = mm(spread[...], affs[...])
    slice_grad = jnp.zeros((WIDTH, SLICES), F32)
    for h in range(HEADS):
        at = h * WIDTH
        part = between[at : at + WIDTH] + soft_col[:, 0:1] * softs[h]
        gproj[C + at : C + at + WIDTH, :] = part.astype(BF16)
        slice_grad = slice_grad + mm(
            proj_in[C + at : C + at + WIDTH, :], affs[h * SLICES : (h + 1) * SLICES, :], NT
        )
    in_grad = mm(normed_in[...], gproj[...], NT)
    for b in range(4):
        grads[b * C : (b + 1) * C, :] = in_grad[:, b * 128 : (b + 1) * 128].astype(grads.dtype)
    tail = jnp.concatenate([slice_grad, jnp.zeros((WIDTH, SLICES), F32)], axis=1)
    grads[6 * C : 6 * C + WIDTH, :] = tail.astype(grads.dtype)
    grads[6 * C + WIDTH :, :] = jnp.zeros((GY * GRAD_ROWS - 6 * C - WIDTH, 128), grads.dtype)

    g_unit = mm(entrance[...], gproj[...]) * gain_col[:, 0:1]
    unit = (xt - mean) * inv
    m1 = jnp.sum(g_unit, axis=0, keepdims=True) * (1.0 / C)
    m2 = jnp.sum(g_unit * unit, axis=0, keepdims=True) * (1.0 / C)
    cell = cot_in[...].astype(F32) + inv * (g_unit - m1 - unit * m2)
    cell_rows = mm(pick[...], cell.astype(BF16), NT).astype(BF16)
    for q in range(GY):
        send[q, 0 : SIN * PIECE, :] = cell_rows[q * 32 : (q + 1) * 32]


def gather_kernel(
    scale, at, r0, r1, r2, r3, grad_in, grad_out, grad_slice, flat, tail, sem
):
    y, core, x = at[0], at[1], at[2]
    for dy, recv in enumerate((r0, r1, r2, r3)):
        for dx in range(4):
            for dc in range(2):
                index = (((y - dy) & 3) * 2 + (core ^ dc)) * 4 + ((x - dx) & 3)
                start = pl.multiple_of(index * GRAD_ROWS, 8)
                flat[pl.ds(start, GRAD_ROWS), :] = recv[dx * 2 + dc].astype(F32) * scale
    tail[...] = flat[6 * C : 6 * C + WIDTH, 0:SLICES]
    copies = []
    for b in range(6):
        out, c = (grad_in, b) if b < 4 else (grad_out, b - 4)
        target = out.at[:, c * 128 : (c + 1) * 128]
        copies.append(pltpu.make_async_copy(flat.at[b * C : (b + 1) * C], target, sem.at[b]))
    copies.append(pltpu.make_async_copy(tail, grad_slice, sem.at[6]))
    for copy in copies:
        copy.start()
    for copy in copies:
        copy.wait()


def unpack_kernel(home, result, cell_grad, cells, rows, sem):
    copies = []
    order = piece_order(True)
    for j in range(8):
        got = jnp.concatenate([home[4 * j + a] for a in range(4)], axis=0)
        moved = mm(order, got).astype(BF16)
        span = pl.ds(16 * j, 16)
        cells[:, span, :] = moved[0 : SIN * 16].reshape(SIN, 16, C)
        rows[:, span, :] = moved[SIN * 16 :].reshape(SOUT, 16, C)
        if j % 2 == 1:
            both = pl.ds(16 * (j - 1), 32)
            pair = [
                pltpu.make_async_copy(cells.at[:, both, :], cell_grad.at[:, both, :], sem.at[j - 1]),
                pltpu.make_async_copy(rows.at[:, both, :], result.at[:, both, :], sem.at[j]),
            ]
            for copy in pair:
                copy.start()
            copies += pair
    for copy in copies:
        copy.wait()


def shards(
    cells, tally, plan, cot, gain, entrance, portion, softness, base,
    request, lookup, content, exit_w,
):
    gain = gain.reshape(1, C)
    softness = softness.reshape(1, WIDTH)
    base = base.reshape(1, HEADS)
    scale = 1.0 / math.sqrt(GX * GY * SIN * BLK)

    def swap(x, axes):
        return lax.all_to_all(x, axes, 0, 0, tiled=True)

    def shifted(x, axis, n, d):
        return lax.ppermute(x, axis, [(i, (i + d) % n) for i in range(n)])

    sent = call(
        pack_kernel,
        sds((GY, TALL, 128), BF16),
        tally, plan, cells.reshape(SIN, BLK, C), cot.reshape(SOUT, BLK, C),
        hbm=True,
        hbm_out=True,
        vmem=62,
        scratch=[
            pltpu.SMEM((1,), jnp.int32),
            pltpu.SMEM((1, SIN), jnp.int32),
            pltpu.VMEM((8, SIN + SOUT, 16, C), BF16),
            pltpu.VMEM((GY, TALL, 128), BF16),
            pltpu.SemaphoreType.DMA((2,)),
            pltpu.SemaphoreType.DMA((8, 2)),
            pltpu.SemaphoreType.DMA((8,)),
        ],
    )
    entrance_t, exit_t, spread, soft_spread, gain_col, base_col, soft_col = call(
        weight_kernel,
        [
            sds((2 * C, C), BF16),
            sds((C, C), BF16),
            sds((C, 512), BF16),
            sds((16, C), BF16),
            sds((C, 128), F32),
            sds((HEADS, 128), F32),
            sds((WIDTH, 128), F32),
        ],
        gain, entrance, portion, softness, base, exit_w,
    )
    recv = swap(sent, ("z", "x"))
    spot = (lax.axis_index("z") * 4 + lax.axis_index("x")).astype(jnp.int32).reshape(1)
    state = call(
        forward_kernel,
        [
            sds((HEADS, TOKEN_ROWS, 128), BF16),
            sds((HOME, ROWS), BF16),
            sds((C, ROWS), BF16),
            sds((C, ROWS), BF16),
            sds((2 * C, ROWS), BF16),
            sds((512, ROWS), F32),
            sds((512, ROWS), F32),
            sds((512, ROWS), BF16),
            sds((C, ROWS), BF16),
            sds((C, ROWS), BF16),
            sds((8, ROWS), F32),
            sds((16, ROWS), F32),
        ],
        spot, recv, entrance_t, exit_w, spread, soft_spread, gain_col, base_col,
        scalars=1,
    )
    token, saved = state[0], state[1:]
    token = swap(token, ("y", "core"))
    token = swap(spread_sum(token, GY, BF16), ("z", "x"))
    mix = call(
        token_kernel, sds((GX, MIX_ROWS, 128), BF16), token, request, lookup, content
    )
    mix = swap(mix, ("y", "core"))
    send, grads = call(
        backward_kernel,
        [sds((GY, SEND, C), BF16), sds((GY * GRAD_ROWS, 128), BF16)],
        mix, entrance, exit_t, spread, gain_col, soft_col, *saved,
        scratch=[
            pltpu.VMEM((2 * C + 16, 512), BF16),
            pltpu.VMEM((2 * C + 16, ROWS), BF16),
            pltpu.VMEM((512, ROWS), F32),
            pltpu.VMEM((512, ROWS), BF16),
            pltpu.VMEM((2 * C, ROWS), BF16),
        ],
    )
    grads = swap(grads.reshape(GY, GRAD_ROWS, 128), ("y", "core", "x"))
    grads = swap(spread_sum(grads, 8, BF16), ("z",))
    grads = spread_sum(grads, 1, BF16)
    send, grads = lax.optimization_barrier((send, grads))
    home = swap(send, ("z", "x"))
    grads = jnp.concatenate([grads, shifted(grads, "core", 2, 1)], axis=0)
    grads = jnp.concatenate([grads] + [shifted(grads, "x", 4, d) for d in (1, 2, 3)], axis=0)
    gathered = [grads] + [shifted(grads, "y", 4, d) for d in (1, 2, 3)]
    at = jnp.stack([lax.axis_index(a) for a in ("y", "core", "x")]).astype(jnp.int32)
    result, cell_grad = call(
        unpack_kernel,
        [sds((SOUT, BLK, C), BF16), sds((SIN, BLK, C), BF16)],
        home,
        hbm_out=True,
        scratch=[
            pltpu.VMEM((SIN, BLK, C), BF16),
            pltpu.VMEM((SOUT, BLK, C), BF16),
            pltpu.SemaphoreType.DMA((8,)),
        ],
    )
    grad_in, grad_out, grad_slice = call(
        lambda *refs: gather_kernel(scale, *refs),
        [sds((C, 2 * C), F32), sds((C, C), F32), sds((WIDTH, SLICES), F32)],
        at, *gathered,
        scalars=1,
        hbm_out=True,
        scratch=[
            pltpu.VMEM((GY * GRAD_ROWS, 128), F32),
            pltpu.VMEM((WIDTH, SLICES), F32),
            pltpu.SemaphoreType.DMA((7,)),
        ],
    )
    result = result.reshape(SOUT * BLK, C)
    cell_grad = cell_grad.reshape(SIN * BLK, C)
    return result, cell_grad, grad_in, grad_out, grad_slice


def solution(mesh):
    grid = Mesh(mesh.devices.reshape(4, 2, 8, 4), ("y", "core", "z", "x"))
    whole = ("y", "core", "z", "x")
    placed = (P(whole, None), P(whole), P(whole, None), P(whole, None)) + (P(),) * 9
    return jax.shard_map(
        shards,
        mesh=grid,
        in_specs=placed,
        out_specs=(P(whole, None), P(whole, None), P(), P(), P()),
        check_vma=False,
    )
```

```python
import math

import jax
import jax.numpy as jnp
from jax import lax
from jax.experimental import pallas as pl
from jax.experimental.pallas import tpu as pltpu
from jax.sharding import Mesh, PartitionSpec as P

C = 256
HEADS = 8
SLICES = 64
WIDTH = 32
BLK = 128
SIN = 8
SOUT = 4
GX = 8
GY = 32
PIECE = BLK // GY
ROWS = GY * SOUT * PIECE
HOME = GY * SIN * PIECE
SEND = (SIN + SOUT) * PIECE
GROUP = 4 * SEND
META = 8
TALL = 2 * SEND + META
TOKEN_ROWS = 40
MIX_ROWS = 48
GRAD_ROWS = 56

norm_eps = 1e-05
slice_eps = 1e-05

F32 = jnp.float32
BF16 = jnp.bfloat16
HI = lax.Precision.HIGHEST
NN = (((1,), (0,)), ((), ()))
NT = (((1,), (1,)), ((), ()))
TN = (((0,), (0,)), ((), ()))


def mm(a, b, dims=NN, precision=None):
    return lax.dot_general(a, b, dims, precision=precision, preferred_element_type=F32)


def iota(shape, dim):
    return lax.broadcasted_iota(jnp.int32, shape, dim)


def call(body, outs, *args, scalars=0, hbm=False, hbm_out=False, scratch=(), vmem=40):
    vm = pl.BlockSpec(memory_space=pltpu.VMEM)
    sm = pl.BlockSpec(memory_space=pltpu.SMEM)
    far = pl.BlockSpec(memory_space=pltpu.HBM)
    single = not isinstance(outs, (list, tuple))
    listed = [outs] if single else list(outs)
    moved = sum(math.prod(a.shape) * a.dtype.itemsize for a in list(args) + listed)
    res = pl.pallas_call(
        body,
        out_shape=listed,
        in_specs=[sm] * scalars + [far if hbm else vm] * (len(args) - scalars),
        out_specs=[far if hbm_out else vm] * len(listed),
        scratch_shapes=list(scratch),
        compiler_params=pltpu.CompilerParams(vmem_limit_bytes=vmem * 2**20),
        cost_estimate=pl.CostEstimate(flops=0, bytes_accessed=moved, transcendentals=0),
    )(*args)
    return res[0] if single else res


def sds(shape, dtype):
    return jax.ShapeDtypeStruct(shape, dtype)


def column(row):
    n = row.shape[1]
    return jnp.sum(jnp.where(iota((n, n), 0) == iota((n, n), 1), row, 0.0), axis=1, keepdims=True)


def piece_order(back):
    sent = iota((GROUP, GROUP), 1 if back else 0)
    kept = iota((GROUP, GROUP), 0 if back else 1)
    part = (
        (sent >= SEND).astype(jnp.int32)
        + (sent >= 2 * SEND).astype(jnp.int32)
        + (sent >= 3 * SEND).astype(jnp.int32)
    )
    within = sent - part * SEND
    source = (within >> 2) * 16 + part * PIECE + (within & 3)
    return (source == kept).astype(F32).astype(BF16)


def pack_kernel(tally, plan, cells, cot, out, sent, out_sem):
    order = piece_order(False)
    block = iota((META, 128), 1) >> 2
    target = jnp.zeros((META, 128), jnp.int32)
    for s in range(SIN):
        target = jnp.where(block == s, plan[0, s], target)
    held = jnp.clip(tally[0] - block * BLK, 0, BLK)
    meta = jnp.where(iota((META, 128), 0) < 4, target, held).astype(F32).astype(BF16)
    for j in range(GY):
        sent[j, 2 * SEND : TALL, :] = meta
    writes = []
    for j in range(8):
        at = slice(16 * j, 16 * j + 16)
        rows = [cells[:, at, :].reshape(16 * SIN, C), cot[:, at, :].reshape(16 * SOUT, C)]
        moved = mm(order, jnp.concatenate(rows, axis=0)).astype(BF16)
        for a in range(4):
            part = moved[a * SEND : (a + 1) * SEND]
            sent[4 * j + a, 0:SEND, :] = part[:, 0:128]
            sent[4 * j + a, SEND : 2 * SEND, :] = part[:, 128:C]
        group = pl.ds(4 * j, 4)
        copy = pltpu.make_async_copy(sent.at[group], out.at[group], out_sem.at[j])
        copy.start()
        writes.append(copy)
    for copy in writes:
        copy.wait()


def weight_kernel(
    gain, entrance, portion, softness, base, exit_w,
    entrance_t, exit_t, spread_out, soft_spread_out, gain_out, base_out, soft_out,
):
    eye = (iota((C, C), 0) == iota((C, C), 1)).astype(F32).astype(BF16)
    entrance_t[...] = mm(entrance[...], eye, TN).astype(BF16)
    exit_t[...] = mm(exit_w[...], eye, TN).astype(BF16)
    tall = ((iota((C, WIDTH), 0) & 31) == iota((C, WIDTH), 1)).astype(F32).astype(BF16)
    broad = ((iota((SLICES, 512), 1) & 63) == iota((SLICES, 512), 0)).astype(F32).astype(BF16)
    spread = mm(mm(tall, portion[...]).astype(BF16), broad)
    same = (iota((C, 512), 0) >> 5) == (iota((C, 512), 1) >> 6)
    spread_out[...] = jnp.where(same, spread, 0.0).astype(BF16)
    soft_row = mm(softness[...], tall, NT)
    soft_same = (iota((16, C), 1) >> 5) == iota((16, C), 0)
    soft_spread_out[...] = jnp.where(soft_same, soft_row, 0.0).astype(BF16)
    gain_out[...] = jnp.broadcast_to(column(gain[...]), (C, 128))
    base_out[...] = jnp.broadcast_to(column(base[...]), (HEADS, 128))
    soft_out[...] = jnp.broadcast_to(column(softness[...].astype(F32)), (WIDTH, 128))


def forward_kernel(
    spot, recv, entrance_t, exit_w, spread, soft_spread, gain_col, base_col,
    token, pick, xt_out, normed_out, proj_out, prob_out, scaled_out, slice_out,
    uns_out, cot_out, rows_out, heads_out,
):
    mine = spot[0]
    cells = jnp.concatenate(
        [recv[:, a : a + SIN * PIECE, :].reshape(HOME, 128) for a in (0, SEND)], axis=1
    )
    cot = jnp.concatenate(
        [recv[:, a + SIN * PIECE : a + SEND, :].reshape(ROWS, 128) for a in (0, SEND)], axis=1
    )
    meta = recv[:, 2 * SEND : TALL, :].astype(F32)
    upper = iota((GY, META, 128), 1) < 4
    target = jnp.max(jnp.where(upper, meta, -1.0), axis=1)
    held = jnp.max(jnp.where(upper, 0.0, meta), axis=1)

    lane = iota((GY, 128), 1)
    lane_f = lane.astype(F32)
    hits = [(target[:, 4 * s : 4 * s + 1] == lane_f).astype(F32) for s in range(SIN)]
    taken = hits[0]
    for s in range(1, SIN):
        taken = taken + hits[s]
    before = (iota((GY, GY), 1) < iota((GY, GY), 0)).astype(F32).astype(BF16)
    place = mm(before, taken.astype(BF16)) + lane_f * SOUT + 1.0
    dest = jnp.zeros((GY, 128), F32)
    for s in range(SIN):
        found = jnp.sum(hits[s] * place, axis=1, keepdims=True)
        dest = jnp.where((lane >> 2) == s, found, dest)
    row_in_block = (mine * PIECE + (lane & 3)).astype(F32)
    dest = jnp.where(row_in_block < held, dest, 0.0) - 1.0
    flip = (iota((128, 128), 0) == iota((128, 128), 1)).astype(F32).astype(BF16)
    slots = mm(flip, dest.astype(BF16), NT)[0:32, :]
    slots = (slots * 4.0 + (iota((32, GY), 0) & 3).astype(F32)).astype(jnp.int32)
    at_row = iota((32, ROWS), 1)
    seen = jnp.zeros((32, ROWS), F32)
    for p in range(GY):
        match = (slots[:, p : p + 1] == at_row).astype(F32)
        seen = seen + match
        pick[p * 32 : (p + 1) * 32, :] = match.astype(BF16)
    live = jnp.sum(seen, axis=0, keepdims=True)

    xt = mm(cells, pick[...], TN)
    xt_out[...] = xt.astype(BF16)
    mean = jnp.sum(xt, axis=0, keepdims=True) * (1.0 / C)
    centered = xt - mean
    var = jnp.sum(centered * centered, axis=0, keepdims=True) * (1.0 / C)
    inv = lax.rsqrt(var + norm_eps)
    normed = (centered * inv * gain_col[:, 0:1]).astype(BF16)
    normed_out[...] = normed
    proj_out[...] = mm(entrance_t[...], normed).astype(BF16)
    rows_out[0:1, :] = live
    rows_out[1:2, :] = mean
    rows_out[2:3, :] = inv

    mid = proj_out[C : 2 * C, :]
    presq = mm(soft_spread[...], mid)[0:HEADS]
    softplus = jnp.maximum(presq, 0.0) + jnp.log1p(jnp.exp(-jnp.abs(presq)))
    inv_temp = 1.0 / (base_col[:, 0:1] + softplus)
    heads_out[0:8, :] = inv_temp
    heads_out[8:16, :] = presq
    scaled_out[...] = mm(spread[...], mid, TN)

    back = mm(exit_w[...], cot, NT) * live
    uns_out[...] = back.astype(BF16)
    eye = (iota((C, C), 0) == iota((C, C), 1)).astype(F32).astype(BF16)
    cot_out[...] = (mm(eye, cot, NT) * live).astype(BF16)

    for h in range(HEADS):
        at = h * SLICES
        scaled = scaled_out[at : at + SLICES, :] * inv_temp[h : h + 1, :]
        scaled_out[at : at + SLICES, :] = scaled
        top = jnp.max(scaled, axis=0, keepdims=True)
        e = jnp.exp(scaled - top)
        prob = e * (1.0 / jnp.sum(e, axis=0, keepdims=True))
        prob_out[at : at + SLICES, :] = prob
        half = (prob * live).astype(BF16)
        slice_out[at : at + SLICES, :] = half
        left = jnp.concatenate(
            [
                proj_out[h * WIDTH : (h + 1) * WIDTH, :],
                uns_out[h * WIDTH : (h + 1) * WIDTH, :],
                jnp.ones((16, ROWS), BF16),
            ],
            axis=0,
        )
        sums = mm(left, half, NT)
        main = jnp.concatenate([sums[0:WIDTH], sums[WIDTH : 2 * WIDTH]], axis=1)
        count = jnp.concatenate([sums[2 * WIDTH : 2 * WIDTH + 8]] * 2, axis=1)
        token[h] = jnp.concatenate([main, count], axis=0).astype(BF16)


def spread_kernel(recv, out):
    n = recv.shape[0]
    total = recv[0].astype(F32)
    for i in range(1, n):
        total = total + recv[i].astype(F32)
    total = total.astype(out.dtype)
    for i in range(out.shape[0]):
        out[i] = total


def spread_sum(recv, copies, dtype):
    return call(spread_kernel, sds((copies,) + recv.shape[1:], dtype), recv)


def token_kernel(recv, request, lookup, content, out):
    total = recv[0].astype(F32)
    for i in range(1, GY):
        total = total + recv[i].astype(F32)
    inverse = 1.0 / (total[WIDTH : WIDTH + 1, 0:SLICES] + slice_eps)
    tok = total[0:WIDTH, 0:SLICES] * inverse
    cot = total[0:WIDTH, SLICES:128]
    scale = WIDTH ** (-0.5)
    q = mm(request[...], tok, TN, HI)
    k = mm(lookup[...], tok, TN, HI)
    v = mm(content[...], tok, TN, HI)
    scores = mm(k, q, TN, HI) * scale
    e = jnp.exp(scores - jnp.max(scores, axis=0, keepdims=True))
    att = e / jnp.sum(e, axis=0, keepdims=True)
    mixed = mm(v, att, NN, HI)
    g_att = mm(v, cot, TN, HI)
    g_v = mm(cot, att, NT, HI)
    g_s = att * (g_att - jnp.sum(att * g_att, axis=0, keepdims=True)) * scale
    g_q = mm(k, g_s, NN, HI)
    g_k = mm(q, g_s, NT, HI)
    g_tok = mm(request[...], g_q, NN, HI)
    g_tok = g_tok + mm(lookup[...], g_k, NN, HI)
    g_tok = g_tok + mm(content[...], g_v, NN, HI)
    g_num = g_tok * inverse
    g_den = -jnp.sum(g_tok * tok, axis=0, keepdims=True) * inverse
    g_den_hi = g_den.astype(BF16).astype(F32)
    g_den_lo = g_den - g_den_hi
    main = jnp.concatenate([mixed, g_num], axis=1).astype(BF16)
    tail = jnp.concatenate([g_den_hi, g_den_lo], axis=1)
    tail = jnp.broadcast_to(tail, (16, 128)).astype(BF16)
    for i in range(GX):
        out[i, 0:WIDTH, :] = main
        out[i, WIDTH:MIX_ROWS, :] = tail


def backward_kernel(
    mix, spread, soft_col, normed_in, proj_in, prob_in, scaled_in, slice_in,
    uns_in, cot_in, rows_in, heads_in,
    grads, gproj, deslice_out, weave, stack, gprob, affs,
):
    live = rows_in[0:1, :]
    weave[...] = jnp.zeros_like(weave)
    lane = iota((WIDTH, 128), 1)
    lane16 = iota((16, 128), 1)
    sub16 = iota((16, 128), 0)
    for h in range(HEADS):
        block = mix[h].astype(F32)
        turned = pltpu.roll(block, SLICES, 1)
        low = h % 2 == 0
        left, right = (block, turned) if low else (turned, block)
        here = (lane < SLICES) if low else (lane >= SLICES)
        at = (h // 2) * 128
        weave[h * WIDTH : (h + 1) * WIDTH, at : at + 128] = jnp.where(
            here, left[0:WIDTH], 0.0
        ).astype(BF16)
        weave[C + h * WIDTH : C + (h + 1) * WIDTH, at : at + 128] = jnp.where(
            here, right[0:WIDTH], 0.0
        ).astype(BF16)
    for g in range(HEADS // 2):
        even = mix[2 * g, WIDTH:MIX_ROWS, :].astype(F32)
        odd = mix[2 * g + 1, WIDTH:MIX_ROWS, :].astype(F32)
        upper = jnp.where(lane16 < SLICES, even, pltpu.roll(odd, SLICES, 1))
        lower = jnp.where(lane16 < SLICES, pltpu.roll(even, SLICES, 1), odd)
        both = jnp.where(sub16 == 0, upper, jnp.where(sub16 == 1, lower, 0.0))
        weave[2 * C : 2 * C + 16, g * 128 : (g + 1) * 128] = both.astype(BF16)
    stack[0:C, :] = uns_in[...]
    stack[C : 2 * C, :] = proj_in[0:C, :]
    stack[2 * C : 2 * C + 16, :] = jnp.ones((16, ROWS), BF16)

    rows = mm(weave[0 : 2 * C, :], slice_in[...])
    deslice = rows[0:C].astype(BF16)
    gproj[0:C, :] = rows[C : 2 * C].astype(BF16)
    gprob[...] = mm(weave[...], stack[...], TN)
    deslice_out[...] = deslice
    out_grad = mm(deslice, cot_in[...], NT)
    for b in range(2):
        grads[(4 + b) * C : (5 + b) * C, :] = out_grad[:, b * 128 : (b + 1) * 128].astype(
            grads.dtype
        )

    softs = []
    for h in range(HEADS):
        at = h * SLICES
        inv_temp = heads_in[h : h + 1, :]
        presq = heads_in[8 + h : 9 + h, :]
        prob = prob_in[at : at + SLICES, :]
        gp = gprob[at : at + SLICES, :] * live
        adj = prob * (gp - jnp.sum(prob * gp, axis=0, keepdims=True))
        affs[at : at + SLICES, :] = (adj * inv_temp).astype(BF16)
        pulled = jnp.sum(adj * scaled_in[at : at + SLICES, :], axis=0, keepdims=True)
        softs.append(-pulled * inv_temp * (1.0 / (1.0 + jnp.exp(-presq))))
    between = mm(spread[...], affs[...])
    slice_grad = jnp.zeros((WIDTH, SLICES), F32)
    for h in range(HEADS):
        at = h * WIDTH
        part = between[at : at + WIDTH] + soft_col[:, 0:1] * softs[h]
        gproj[C + at : C + at + WIDTH, :] = part.astype(BF16)
        slice_grad = slice_grad + mm(
            proj_in[C + at : C + at + WIDTH, :], affs[h * SLICES : (h + 1) * SLICES, :], NT
        )
    in_grad = mm(normed_in[...], gproj[...], NT)
    for b in range(4):
        grads[b * C : (b + 1) * C, :] = in_grad[:, b * 128 : (b + 1) * 128].astype(grads.dtype)
    tail = jnp.concatenate([slice_grad, jnp.zeros((WIDTH, SLICES), F32)], axis=1)
    grads[6 * C : 6 * C + WIDTH, :] = tail.astype(grads.dtype)
    grads[6 * C + WIDTH :, :] = jnp.zeros((GY * GRAD_ROWS - 6 * C - WIDTH, 128), grads.dtype)


def home_kernel(
    entrance, exit_t, gain_col, pick, xt_in, cot_in, rows_in, gproj, deslice, send
):
    live = rows_in[0:1, :]
    mean = rows_in[1:2, :]
    inv = rows_in[2:3, :]
    xt = xt_in[...].astype(F32)
    result = (live * (xt + mm(exit_t[...], deslice[...]))).astype(BF16)
    eye = (iota((ROWS, ROWS), 0) == iota((ROWS, ROWS), 1)).astype(F32).astype(BF16)
    result_rows = mm(eye, result, NT).astype(BF16)
    for q in range(GY):
        send[q, SIN * PIECE : SEND, :] = result_rows[q * 16 : (q + 1) * 16]
    g_unit = mm(entrance[...], gproj[...]) * gain_col[:, 0:1]
    unit = (xt - mean) * inv
    m1 = jnp.sum(g_unit, axis=0, keepdims=True) * (1.0 / C)
    m2 = jnp.sum(g_unit * unit, axis=0, keepdims=True) * (1.0 / C)
    cell = cot_in[...].astype(F32) + inv * (g_unit - m1 - unit * m2)
    cell_rows = mm(pick[...], cell.astype(BF16), NT).astype(BF16)
    for q in range(GY):
        send[q, 0 : SIN * PIECE, :] = cell_rows[q * 32 : (q + 1) * 32]


def gather_kernel(
    scale, at, r0, r1, grad_in, grad_out, grad_slice, flat, tail, sem
):
    y, core, x = at[0], at[1], at[2]
    for dc, recv in enumerate((r0, r1)):
        for dy in range(4):
            for dx in range(4):
                index = (((y - dy) & 3) * 2 + (core ^ dc)) * 4 + ((x - dx) & 3)
                start = pl.multiple_of(index * GRAD_ROWS, 8)
                flat[pl.ds(start, GRAD_ROWS), :] = recv[dy * 4 + dx].astype(F32) * scale
    tail[...] = flat[6 * C : 6 * C + WIDTH, 0:SLICES]
    copies = []
    for b in range(6):
        out, c = (grad_in, b) if b < 4 else (grad_out, b - 4)
        target = out.at[:, c * 128 : (c + 1) * 128]
        copies.append(pltpu.make_async_copy(flat.at[b * C : (b + 1) * C], target, sem.at[b]))
    copies.append(pltpu.make_async_copy(tail, grad_slice, sem.at[6]))
    for copy in copies:
        copy.start()
    for copy in copies:
        copy.wait()


def unpack_kernel(home, result, cell_grad, cells, rows, sem):
    copies = []
    order = piece_order(True)
    for j in range(8):
        got = jnp.concatenate([home[4 * j + a] for a in range(4)], axis=0)
        moved = mm(order, got).astype(BF16)
        span = pl.ds(16 * j, 16)
        cells[:, span, :] = moved[0 : SIN * 16].reshape(SIN, 16, C)
        rows[:, span, :] = moved[SIN * 16 :].reshape(SOUT, 16, C)
        if j % 2 == 1:
            both = pl.ds(16 * (j - 1), 32)
            pair = [
                pltpu.make_async_copy(cells.at[:, both, :], cell_grad.at[:, both, :], sem.at[j - 1]),
                pltpu.make_async_copy(rows.at[:, both, :], result.at[:, both, :], sem.at[j]),
            ]
            for copy in pair:
                copy.start()
            copies += pair
    for copy in copies:
        copy.wait()


def shards(
    cells, tally, plan, cot, gain, entrance, portion, softness, base,
    request, lookup, content, exit_w,
):
    gain = gain.reshape(1, C)
    softness = softness.reshape(1, WIDTH)
    base = base.reshape(1, HEADS)
    scale = 1.0 / math.sqrt(GX * GY * SIN * BLK)

    def swap(x, axes):
        return lax.all_to_all(x, axes, 0, 0, tiled=True)

    def shifted(x, axis, n, d):
        return lax.ppermute(x, axis, [(i, (i + d) % n) for i in range(n)])

    sent = call(
        pack_kernel,
        sds((GY, TALL, 128), BF16),
        tally, plan, cells.reshape(SIN, BLK, C), cot.reshape(SOUT, BLK, C),
        scalars=2,
        hbm_out=True,
        vmem=62,
        scratch=[
            pltpu.VMEM((GY, TALL, 128), BF16),
            pltpu.SemaphoreType.DMA((8,)),
        ],
    )
    entrance_t, exit_t, spread, soft_spread, gain_col, base_col, soft_col = call(
        weight_kernel,
        [
            sds((2 * C, C), BF16),
            sds((C, C), BF16),
            sds((C, 512), BF16),
            sds((16, C), BF16),
            sds((C, 128), F32),
            sds((HEADS, 128), F32),
            sds((WIDTH, 128), F32),
        ],
        gain, entrance, portion, softness, base, exit_w,
    )
    recv = swap(sent, ("z", "x"))
    spot = (lax.axis_index("z") * 4 + lax.axis_index("x")).astype(jnp.int32).reshape(1)
    state = call(
        forward_kernel,
        [
            sds((HEADS, TOKEN_ROWS, 128), BF16),
            sds((HOME, ROWS), BF16),
            sds((C, ROWS), BF16),
            sds((C, ROWS), BF16),
            sds((2 * C, ROWS), BF16),
            sds((512, ROWS), F32),
            sds((512, ROWS), F32),
            sds((512, ROWS), BF16),
            sds((C, ROWS), BF16),
            sds((C, ROWS), BF16),
            sds((8, ROWS), F32),
            sds((16, ROWS), F32),
        ],
        spot, recv, entrance_t, exit_w, spread, soft_spread, gain_col, base_col,
        scalars=1,
    )
    token, pick, xt, normed, proj, prob, scaled, slices, uns, cot_t, rows, heads = state
    token = swap(token, ("y", "core"))
    token = swap(spread_sum(token, GY, BF16), ("z", "x"))
    mix = call(
        token_kernel, sds((GX, MIX_ROWS, 128), BF16), token, request, lookup, content
    )
    mix = swap(mix, ("y", "core"))
    grads, gproj, deslice = call(
        backward_kernel,
        [
            sds((GY * GRAD_ROWS, 128), BF16),
            sds((2 * C, ROWS), BF16),
            sds((C, ROWS), BF16),
        ],
        mix, spread, soft_col, normed, proj, prob, scaled, slices, uns, cot_t, rows, heads,
        scratch=[
            pltpu.VMEM((2 * C + 16, 512), BF16),
            pltpu.VMEM((2 * C + 16, ROWS), BF16),
            pltpu.VMEM((512, ROWS), F32),
            pltpu.VMEM((512, ROWS), BF16),
        ],
    )
    send = call(
        home_kernel,
        sds((GY, SEND, C), BF16),
        entrance, exit_t, gain_col, pick, xt, cot_t, rows, gproj, deslice,
    )
    grads = swap(grads.reshape(GY, GRAD_ROWS, 128), ("y", "core", "x"))
    grads = swap(spread_sum(grads, 8, BF16), ("z",))
    grads = spread_sum(grads, 1, BF16)
    send, grads = lax.optimization_barrier((send, grads))
    home = swap(send, ("z", "x"))
    for axis in ("x", "y"):
        grads = jnp.concatenate([grads] + [shifted(grads, axis, 4, d) for d in (1, 2, 3)], axis=0)
    gathered = [grads, shifted(grads, "core", 2, 1)]
    at = jnp.stack([lax.axis_index(a) for a in ("y", "core", "x")]).astype(jnp.int32)
    result, cell_grad = call(
        unpack_kernel,
        [sds((SOUT, BLK, C), BF16), sds((SIN, BLK, C), BF16)],
        home,
        hbm_out=True,
        scratch=[
            pltpu.VMEM((SIN, BLK, C), BF16),
            pltpu.VMEM((SOUT, BLK, C), BF16),
            pltpu.SemaphoreType.DMA((8,)),
        ],
    )
    grad_in, grad_out, grad_slice = call(
        lambda *refs: gather_kernel(scale, *refs),
        [sds((C, 2 * C), F32), sds((C, C), F32), sds((WIDTH, SLICES), F32)],
        at, *gathered,
        scalars=1,
        hbm_out=True,
        scratch=[
            pltpu.VMEM((GY * GRAD_ROWS, 128), F32),
            pltpu.VMEM((WIDTH, SLICES), F32),
            pltpu.SemaphoreType.DMA((7,)),
        ],
    )
    result = result.reshape(SOUT * BLK, C)
    cell_grad = cell_grad.reshape(SIN * BLK, C)
    return result, cell_grad, grad_in, grad_out, grad_slice


def solution(mesh):
    grid = Mesh(mesh.devices.reshape(4, 2, 8, 4), ("y", "core", "z", "x"))
    whole = ("y", "core", "z", "x")
    placed = (P(whole, None), P(whole), P(whole, None), P(whole, None)) + (P(),) * 9
    return jax.shard_map(
        shards,
        mesh=grid,
        in_specs=placed,
        out_specs=(P(whole, None), P(whole, None), P(), P(), P()),
        check_vma=False,
    )
```

```python
import math

import jax
import jax.numpy as jnp
from jax import lax
from jax.experimental import pallas as pl
from jax.experimental.pallas import tpu as pltpu
from jax.sharding import Mesh, PartitionSpec as P

C = 256
HEADS = 8
SLICES = 64
WIDTH = 32
BLK = 128
SIN = 8
SOUT = 4
GX = 8
GY = 32
PIECE = BLK // GY
ROWS = GY * SOUT * PIECE
HOME = GY * SIN * PIECE
SEND = (SIN + SOUT) * PIECE
GROUP = 4 * SEND
META = 8
TALL = 2 * SEND + META
TOKEN_ROWS = 40
MIX_ROWS = 48
GRAD_ROWS = 56

norm_eps = 1e-05
slice_eps = 1e-05

F32 = jnp.float32
BF16 = jnp.bfloat16
HI = lax.Precision.HIGHEST
NN = (((1,), (0,)), ((), ()))
NT = (((1,), (1,)), ((), ()))
TN = (((0,), (0,)), ((), ()))


def mm(a, b, dims=NN, precision=None):
    return lax.dot_general(a, b, dims, precision=precision, preferred_element_type=F32)


def iota(shape, dim):
    return lax.broadcasted_iota(jnp.int32, shape, dim)


def call(body, outs, *args, scalars=0, hbm=False, hbm_out=False, scratch=(), vmem=40):
    vm = pl.BlockSpec(memory_space=pltpu.VMEM)
    sm = pl.BlockSpec(memory_space=pltpu.SMEM)
    far = pl.BlockSpec(memory_space=pltpu.HBM)
    single = not isinstance(outs, (list, tuple))
    listed = [outs] if single else list(outs)
    moved = sum(math.prod(a.shape) * a.dtype.itemsize for a in list(args) + listed)
    res = pl.pallas_call(
        body,
        out_shape=listed,
        in_specs=[sm] * scalars + [far if hbm else vm] * (len(args) - scalars),
        out_specs=[far if hbm_out else vm] * len(listed),
        scratch_shapes=list(scratch),
        compiler_params=pltpu.CompilerParams(vmem_limit_bytes=vmem * 2**20),
        cost_estimate=pl.CostEstimate(flops=0, bytes_accessed=moved, transcendentals=0),
    )(*args)
    return res[0] if single else res


def sds(shape, dtype):
    return jax.ShapeDtypeStruct(shape, dtype)


def column(row):
    n = row.shape[1]
    return jnp.sum(jnp.where(iota((n, n), 0) == iota((n, n), 1), row, 0.0), axis=1, keepdims=True)


def piece_order(back):
    sent = iota((GROUP, GROUP), 1 if back else 0)
    kept = iota((GROUP, GROUP), 0 if back else 1)
    part = (
        (sent >= SEND).astype(jnp.int32)
        + (sent >= 2 * SEND).astype(jnp.int32)
        + (sent >= 3 * SEND).astype(jnp.int32)
    )
    within = sent - part * SEND
    source = (within >> 2) * 16 + part * PIECE + (within & 3)
    return (source == kept).astype(F32).astype(BF16)


def pack_kernel(tally, plan, cells, cot, out, sent, out_sem):
    order = piece_order(False)
    block = iota((META, 128), 1) >> 2
    target = jnp.zeros((META, 128), jnp.int32)
    for s in range(SIN):
        target = jnp.where(block == s, plan[0, s], target)
    held = jnp.clip(tally[0] - block * BLK, 0, BLK)
    meta = jnp.where(iota((META, 128), 0) < 4, target, held).astype(F32).astype(BF16)
    for j in range(GY):
        sent[j, 2 * SEND : TALL, :] = meta
    writes = []
    for j in range(8):
        at = slice(16 * j, 16 * j + 16)
        rows = [cells[:, at, :].reshape(16 * SIN, C), cot[:, at, :].reshape(16 * SOUT, C)]
        moved = mm(order, jnp.concatenate(rows, axis=0)).astype(BF16)
        for a in range(4):
            part = moved[a * SEND : (a + 1) * SEND]
            sent[4 * j + a, 0:SEND, :] = part[:, 0:128]
            sent[4 * j + a, SEND : 2 * SEND, :] = part[:, 128:C]
        group = pl.ds(4 * j, 4)
        copy = pltpu.make_async_copy(sent.at[group], out.at[group], out_sem.at[j])
        copy.start()
        writes.append(copy)
    for copy in writes:
        copy.wait()


def weight_kernel(
    gain, entrance, portion, softness, base, exit_w,
    entrance_t, exit_t, spread_out, soft_spread_out, gain_out, base_out, soft_out,
):
    eye = (iota((C, C), 0) == iota((C, C), 1)).astype(F32).astype(BF16)
    entrance_t[...] = mm(entrance[...], eye, TN).astype(BF16)
    exit_t[...] = mm(exit_w[...], eye, TN).astype(BF16)
    tall = ((iota((C, WIDTH), 0) & 31) == iota((C, WIDTH), 1)).astype(F32).astype(BF16)
    broad = ((iota((SLICES, 512), 1) & 63) == iota((SLICES, 512), 0)).astype(F32).astype(BF16)
    spread = mm(mm(tall, portion[...]).astype(BF16), broad)
    same = (iota((C, 512), 0) >> 5) == (iota((C, 512), 1) >> 6)
    spread_out[...] = jnp.where(same, spread, 0.0).astype(BF16)
    soft_row = mm(softness[...], tall, NT)
    soft_same = (iota((16, C), 1) >> 5) == iota((16, C), 0)
    soft_spread_out[...] = jnp.where(soft_same, soft_row, 0.0).astype(BF16)
    gain_out[...] = jnp.broadcast_to(column(gain[...]), (C, 128))
    base_out[...] = jnp.broadcast_to(column(base[...]), (HEADS, 128))
    soft_out[...] = jnp.broadcast_to(column(softness[...].astype(F32)), (WIDTH, 128))


def forward_kernel(
    spot, recv, entrance_t, exit_w, spread, soft_spread, gain_col, base_col,
    token, pick, xt_out, normed_out, proj_out, prob_out, scaled_out, slice_out,
    uns_out, cot_out, rows_out, heads_out,
):
    mine = spot[0]
    cells = jnp.concatenate(
        [recv[:, a : a + SIN * PIECE, :].reshape(HOME, 128) for a in (0, SEND)], axis=1
    )
    cot = jnp.concatenate(
        [recv[:, a + SIN * PIECE : a + SEND, :].reshape(ROWS, 128) for a in (0, SEND)], axis=1
    )
    meta = recv[:, 2 * SEND : TALL, :].astype(F32)
    upper = iota((GY, META, 128), 1) < 4
    target = jnp.max(jnp.where(upper, meta, -1.0), axis=1)
    held = jnp.max(jnp.where(upper, 0.0, meta), axis=1)

    lane = iota((GY, 128), 1)
    lane_f = lane.astype(F32)
    hits = [(target[:, 4 * s : 4 * s + 1] == lane_f).astype(F32) for s in range(SIN)]
    taken = hits[0]
    for s in range(1, SIN):
        taken = taken + hits[s]
    before = (iota((GY, GY), 1) < iota((GY, GY), 0)).astype(F32).astype(BF16)
    place = mm(before, taken.astype(BF16)) + lane_f * SOUT + 1.0
    dest = jnp.zeros((GY, 128), F32)
    for s in range(SIN):
        found = jnp.sum(hits[s] * place, axis=1, keepdims=True)
        dest = jnp.where((lane >> 2) == s, found, dest)
    row_in_block = (mine * PIECE + (lane & 3)).astype(F32)
    dest = jnp.where(row_in_block < held, dest, 0.0) - 1.0
    flip = (iota((128, 128), 0) == iota((128, 128), 1)).astype(F32).astype(BF16)
    slots = mm(flip, dest.astype(BF16), NT)[0:32, :]
    slots = (slots * 4.0 + (iota((32, GY), 0) & 3).astype(F32)).astype(jnp.int32)
    at_row = iota((32, ROWS), 1)
    seen = jnp.zeros((32, ROWS), F32)
    for p in range(GY):
        match = (slots[:, p : p + 1] == at_row).astype(F32)
        seen = seen + match
        pick[p * 32 : (p + 1) * 32, :] = match.astype(BF16)
    live = jnp.sum(seen, axis=0, keepdims=True)

    xt = mm(cells, pick[...], TN)
    xt_out[...] = xt.astype(BF16)
    mean = jnp.sum(xt, axis=0, keepdims=True) * (1.0 / C)
    centered = xt - mean
    var = jnp.sum(centered * centered, axis=0, keepdims=True) * (1.0 / C)
    inv = lax.rsqrt(var + norm_eps)
    normed = (centered * inv * gain_col[:, 0:1]).astype(BF16)
    normed_out[...] = normed
    proj_out[...] = mm(entrance_t[...], normed).astype(BF16)
    rows_out[0:1, :] = live
    rows_out[1:2, :] = mean
    rows_out[2:3, :] = inv

    mid = proj_out[C : 2 * C, :]
    presq = mm(soft_spread[...], mid)[0:HEADS]
    softplus = jnp.maximum(presq, 0.0) + jnp.log1p(jnp.exp(-jnp.abs(presq)))
    inv_temp = 1.0 / (base_col[:, 0:1] + softplus)
    heads_out[0:8, :] = inv_temp
    heads_out[8:16, :] = presq
    scaled_out[...] = mm(spread[...], mid, TN)

    back = mm(exit_w[...], cot, NT) * live
    uns_out[...] = back.astype(BF16)
    eye = (iota((C, C), 0) == iota((C, C), 1)).astype(F32).astype(BF16)
    cot_out[...] = (mm(eye, cot, NT) * live).astype(BF16)

    for h in range(HEADS):
        at = h * SLICES
        scaled = scaled_out[at : at + SLICES, :] * inv_temp[h : h + 1, :]
        scaled_out[at : at + SLICES, :] = scaled
        top = jnp.max(scaled, axis=0, keepdims=True)
        e = jnp.exp(scaled - top)
        prob = e * (1.0 / jnp.sum(e, axis=0, keepdims=True))
        prob_out[at : at + SLICES, :] = prob
        half = (prob * live).astype(BF16)
        slice_out[at : at + SLICES, :] = half
        left = jnp.concatenate(
            [
                proj_out[h * WIDTH : (h + 1) * WIDTH, :],
                uns_out[h * WIDTH : (h + 1) * WIDTH, :],
                jnp.ones((16, ROWS), BF16),
            ],
            axis=0,
        )
        sums = mm(left, half, NT)
        main = jnp.concatenate([sums[0:WIDTH], sums[WIDTH : 2 * WIDTH]], axis=1)
        count = jnp.concatenate([sums[2 * WIDTH : 2 * WIDTH + 8]] * 2, axis=1)
        token[h] = jnp.concatenate([main, count], axis=0).astype(BF16)


def spread_kernel(recv, out):
    n = recv.shape[0]
    total = recv[0].astype(F32)
    for i in range(1, n):
        total = total + recv[i].astype(F32)
    total = total.astype(out.dtype)
    for i in range(out.shape[0]):
        out[i] = total


def spread_sum(recv, copies, dtype):
    return call(spread_kernel, sds((copies,) + recv.shape[1:], dtype), recv)


def token_kernel(recv, request, lookup, content, out):
    total = recv[0].astype(F32)
    for i in range(1, GY):
        total = total + recv[i].astype(F32)
    inverse = 1.0 / (total[WIDTH : WIDTH + 1, 0:SLICES] + slice_eps)
    tok = total[0:WIDTH, 0:SLICES] * inverse
    cot = total[0:WIDTH, SLICES:128]
    scale = WIDTH ** (-0.5)
    q = mm(request[...], tok, TN, HI)
    k = mm(lookup[...], tok, TN, HI)
    v = mm(content[...], tok, TN, HI)
    scores = mm(k, q, TN, HI) * scale
    e = jnp.exp(scores - jnp.max(scores, axis=0, keepdims=True))
    att = e / jnp.sum(e, axis=0, keepdims=True)
    mixed = mm(v, att, NN, HI)
    g_att = mm(v, cot, TN, HI)
    g_v = mm(cot, att, NT, HI)
    g_s = att * (g_att - jnp.sum(att * g_att, axis=0, keepdims=True)) * scale
    g_q = mm(k, g_s, NN, HI)
    g_k = mm(q, g_s, NT, HI)
    g_tok = mm(request[...], g_q, NN, HI)
    g_tok = g_tok + mm(lookup[...], g_k, NN, HI)
    g_tok = g_tok + mm(content[...], g_v, NN, HI)
    g_num = g_tok * inverse
    g_den = -jnp.sum(g_tok * tok, axis=0, keepdims=True) * inverse
    g_den_hi = g_den.astype(BF16).astype(F32)
    g_den_lo = g_den - g_den_hi
    main = jnp.concatenate([mixed, g_num], axis=1).astype(BF16)
    tail = jnp.concatenate([g_den_hi, g_den_lo], axis=1)
    tail = jnp.broadcast_to(tail, (16, 128)).astype(BF16)
    for i in range(GX):
        out[i, 0:WIDTH, :] = main
        out[i, WIDTH:MIX_ROWS, :] = tail


def backward_kernel(
    mix, spread, soft_col, normed_in, proj_in, prob_in, scaled_in, slice_in,
    uns_in, cot_in, rows_in, heads_in,
    grads, gproj, deslice_out, weave, stack, gprob, affs,
):
    live = rows_in[0:1, :]
    weave[...] = jnp.zeros_like(weave)
    lane = iota((WIDTH, 128), 1)
    lane16 = iota((16, 128), 1)
    sub16 = iota((16, 128), 0)
    for h in range(HEADS):
        block = mix[h].astype(F32)
        turned = pltpu.roll(block, SLICES, 1)
        low = h % 2 == 0
        left, right = (block, turned) if low else (turned, block)
        here = (lane < SLICES) if low else (lane >= SLICES)
        at = (h // 2) * 128
        weave[h * WIDTH : (h + 1) * WIDTH, at : at + 128] = jnp.where(
            here, left[0:WIDTH], 0.0
        ).astype(BF16)
        weave[C + h * WIDTH : C + (h + 1) * WIDTH, at : at + 128] = jnp.where(
            here, right[0:WIDTH], 0.0
        ).astype(BF16)
    for g in range(HEADS // 2):
        even = mix[2 * g, WIDTH:MIX_ROWS, :].astype(F32)
        odd = mix[2 * g + 1, WIDTH:MIX_ROWS, :].astype(F32)
        upper = jnp.where(lane16 < SLICES, even, pltpu.roll(odd, SLICES, 1))
        lower = jnp.where(lane16 < SLICES, pltpu.roll(even, SLICES, 1), odd)
        both = jnp.where(sub16 == 0, upper, jnp.where(sub16 == 1, lower, 0.0))
        weave[2 * C : 2 * C + 16, g * 128 : (g + 1) * 128] = both.astype(BF16)
    stack[0:C, :] = uns_in[...]
    stack[C : 2 * C, :] = proj_in[0:C, :]
    stack[2 * C : 2 * C + 16, :] = jnp.ones((16, ROWS), BF16)

    rows = mm(weave[0 : 2 * C, :], slice_in[...])
    deslice = rows[0:C].astype(BF16)
    gproj[0:C, :] = rows[C : 2 * C].astype(BF16)
    gprob[...] = mm(weave[...], stack[...], TN)
    deslice_out[...] = deslice
    out_grad = mm(deslice, cot_in[...], NT)
    for b in range(2):
        grads[(4 + b) * C : (5 + b) * C, :] = out_grad[:, b * 128 : (b + 1) * 128].astype(
            grads.dtype
        )

    softs = []
    for h in range(HEADS):
        at = h * SLICES
        inv_temp = heads_in[h : h + 1, :]
        presq = heads_in[8 + h : 9 + h, :]
        prob = prob_in[at : at + SLICES, :]
        gp = gprob[at : at + SLICES, :] * live
        adj = prob * (gp - jnp.sum(prob * gp, axis=0, keepdims=True))
        affs[at : at + SLICES, :] = (adj * inv_temp).astype(BF16)
        pulled = jnp.sum(adj * scaled_in[at : at + SLICES, :], axis=0, keepdims=True)
        softs.append(-pulled * inv_temp * (1.0 / (1.0 + jnp.exp(-presq))))
    between = mm(spread[...], affs[...])
    slice_grad = jnp.zeros((WIDTH, SLICES), F32)
    for h in range(HEADS):
        at = h * WIDTH
        part = between[at : at + WIDTH] + soft_col[:, 0:1] * softs[h]
        gproj[C + at : C + at + WIDTH, :] = part.astype(BF16)
        slice_grad = slice_grad + mm(
            proj_in[C + at : C + at + WIDTH, :], affs[h * SLICES : (h + 1) * SLICES, :], NT
        )
    in_grad = mm(normed_in[...], gproj[...], NT)
    for b in range(4):
        grads[b * C : (b + 1) * C, :] = in_grad[:, b * 128 : (b + 1) * 128].astype(grads.dtype)
    tail = jnp.concatenate([slice_grad, jnp.zeros((WIDTH, SLICES), F32)], axis=1)
    grads[6 * C : 6 * C + WIDTH, :] = tail.astype(grads.dtype)
    grads[6 * C + WIDTH :, :] = jnp.zeros((GY * GRAD_ROWS - 6 * C - WIDTH, 128), grads.dtype)


def home_kernel(
    entrance, exit_t, gain_col, pick, xt_in, cot_in, rows_in, gproj, deslice, send
):
    live = rows_in[0:1, :]
    mean = rows_in[1:2, :]
    inv = rows_in[2:3, :]
    xt = xt_in[...].astype(F32)
    result = (live * (xt + mm(exit_t[...], deslice[...]))).astype(BF16)
    eye = (iota((ROWS, ROWS), 0) == iota((ROWS, ROWS), 1)).astype(F32).astype(BF16)
    result_rows = mm(eye, result, NT).astype(BF16)
    for q in range(GY):
        send[q, SIN * PIECE : SEND, :] = result_rows[q * 16 : (q + 1) * 16]
    g_unit = mm(entrance[...], gproj[...]) * gain_col[:, 0:1]
    unit = (xt - mean) * inv
    m1 = jnp.sum(g_unit, axis=0, keepdims=True) * (1.0 / C)
    m2 = jnp.sum(g_unit * unit, axis=0, keepdims=True) * (1.0 / C)
    cell = cot_in[...].astype(F32) + inv * (g_unit - m1 - unit * m2)
    cell_rows = mm(pick[...], cell.astype(BF16), NT).astype(BF16)
    for q in range(GY):
        send[q, 0 : SIN * PIECE, :] = cell_rows[q * 32 : (q + 1) * 32]


def gather_kernel(
    scale, at, r0, r1, grad_in, grad_out, grad_slice, flat, tail, sem
):
    y, core, x = at[0], at[1], at[2]
    for dc, recv in enumerate((r0, r1)):
        for dy in range(4):
            for dx in range(4):
                index = (((y - dy) & 3) * 2 + (core ^ dc)) * 4 + ((x - dx) & 3)
                start = pl.multiple_of(index * GRAD_ROWS, 8)
                flat[pl.ds(start, GRAD_ROWS), :] = recv[dy * 4 + dx].astype(F32) * scale
    tail[...] = flat[6 * C : 6 * C + WIDTH, 0:SLICES]
    copies = []
    for b in range(6):
        out, c = (grad_in, b) if b < 4 else (grad_out, b - 4)
        target = out.at[:, c * 128 : (c + 1) * 128]
        copies.append(pltpu.make_async_copy(flat.at[b * C : (b + 1) * C], target, sem.at[b]))
    copies.append(pltpu.make_async_copy(tail, grad_slice, sem.at[6]))
    for copy in copies:
        copy.start()
    for copy in copies:
        copy.wait()


def unpack_kernel(home, result, cell_grad, cells, rows, sem):
    copies = []
    order = piece_order(True)
    for j in range(8):
        got = jnp.concatenate([home[4 * j + a] for a in range(4)], axis=0)
        moved = mm(order, got).astype(BF16)
        span = pl.ds(16 * j, 16)
        cells[:, span, :] = moved[0 : SIN * 16].reshape(SIN, 16, C)
        rows[:, span, :] = moved[SIN * 16 :].reshape(SOUT, 16, C)
        if j % 2 == 1:
            both = pl.ds(16 * (j - 1), 32)
            pair = [
                pltpu.make_async_copy(cells.at[:, both, :], cell_grad.at[:, both, :], sem.at[j - 1]),
                pltpu.make_async_copy(rows.at[:, both, :], result.at[:, both, :], sem.at[j]),
            ]
            for copy in pair:
                copy.start()
            copies += pair
    for copy in copies:
        copy.wait()


def shards(
    cells, tally, plan, cot, gain, entrance, portion, softness, base,
    request, lookup, content, exit_w,
):
    gain = gain.reshape(1, C)
    softness = softness.reshape(1, WIDTH)
    base = base.reshape(1, HEADS)
    scale = 1.0 / math.sqrt(GX * GY * SIN * BLK)

    def swap(x, axes):
        return lax.all_to_all(x, axes, 0, 0, tiled=True)

    def shifted(x, axis, n, d):
        return lax.ppermute(x, axis, [(i, (i + d) % n) for i in range(n)])

    sent = call(
        pack_kernel,
        sds((GY, TALL, 128), BF16),
        tally, plan, cells.reshape(SIN, BLK, C), cot.reshape(SOUT, BLK, C),
        scalars=2,
        hbm_out=True,
        vmem=62,
        scratch=[
            pltpu.VMEM((GY, TALL, 128), BF16),
            pltpu.SemaphoreType.DMA((8,)),
        ],
    )
    entrance_t, exit_t, spread, soft_spread, gain_col, base_col, soft_col = call(
        weight_kernel,
        [
            sds((2 * C, C), BF16),
            sds((C, C), BF16),
            sds((C, 512), BF16),
            sds((16, C), BF16),
            sds((C, 128), F32),
            sds((HEADS, 128), F32),
            sds((WIDTH, 128), F32),
        ],
        gain, entrance, portion, softness, base, exit_w,
    )
    recv = swap(sent, ("z", "x"))
    spot = (lax.axis_index("z") * 4 + lax.axis_index("x")).astype(jnp.int32).reshape(1)
    state = call(
        forward_kernel,
        [
            sds((HEADS, TOKEN_ROWS, 128), BF16),
            sds((HOME, ROWS), BF16),
            sds((C, ROWS), BF16),
            sds((C, ROWS), BF16),
            sds((2 * C, ROWS), BF16),
            sds((512, ROWS), F32),
            sds((512, ROWS), F32),
            sds((512, ROWS), BF16),
            sds((C, ROWS), BF16),
            sds((C, ROWS), BF16),
            sds((8, ROWS), F32),
            sds((16, ROWS), F32),
        ],
        spot, recv, entrance_t, exit_w, spread, soft_spread, gain_col, base_col,
        scalars=1,
    )
    token, pick, xt, normed, proj, prob, scaled, slices, uns, cot_t, rows, heads = state
    token = swap(token, ("y", "core"))
    token = swap(spread_sum(token, GY, BF16), ("z", "x"))
    mix = call(
        token_kernel, sds((GX, MIX_ROWS, 128), BF16), token, request, lookup, content
    )
    mix = swap(mix, ("y", "core"))
    grads, gproj, deslice = call(
        backward_kernel,
        [
            sds((GY * GRAD_ROWS, 128), BF16),
            sds((2 * C, ROWS), BF16),
            sds((C, ROWS), BF16),
        ],
        mix, spread, soft_col, normed, proj, prob, scaled, slices, uns, cot_t, rows, heads,
        scratch=[
            pltpu.VMEM((2 * C + 16, 512), BF16),
            pltpu.VMEM((2 * C + 16, ROWS), BF16),
            pltpu.VMEM((512, ROWS), F32),
            pltpu.VMEM((512, ROWS), BF16),
        ],
    )
    send = call(
        home_kernel,
        sds((GY, SEND, C), BF16),
        entrance, exit_t, gain_col, pick, xt, cot_t, rows, gproj, deslice,
    )
    grads = swap(grads.reshape(GY, GRAD_ROWS, 128), ("y", "core", "x"))
    grads = spread_sum(grads, 8, BF16)
    send, grads = lax.optimization_barrier((send, grads))
    grads = swap(grads, ("z",))
    grads = spread_sum(grads, 1, BF16)
    send, grads = lax.optimization_barrier((send, grads))
    home = swap(send, ("z", "x"))
    for axis in ("x", "y"):
        grads = jnp.concatenate([grads] + [shifted(grads, axis, 4, d) for d in (1, 2, 3)], axis=0)
    gathered = [grads, shifted(grads, "core", 2, 1)]
    at = jnp.stack([lax.axis_index(a) for a in ("y", "core", "x")]).astype(jnp.int32)
    result, cell_grad = call(
        unpack_kernel,
        [sds((SOUT, BLK, C), BF16), sds((SIN, BLK, C), BF16)],
        home,
        hbm_out=True,
        scratch=[
            pltpu.VMEM((SIN, BLK, C), BF16),
            pltpu.VMEM((SOUT, BLK, C), BF16),
            pltpu.SemaphoreType.DMA((8,)),
        ],
    )
    grad_in, grad_out, grad_slice = call(
        lambda *refs: gather_kernel(scale, *refs),
        [sds((C, 2 * C), F32), sds((C, C), F32), sds((WIDTH, SLICES), F32)],
        at, *gathered,
        scalars=1,
        hbm_out=True,
        scratch=[
            pltpu.VMEM((GY * GRAD_ROWS, 128), F32),
            pltpu.VMEM((WIDTH, SLICES), F32),
            pltpu.SemaphoreType.DMA((7,)),
        ],
    )
    result = result.reshape(SOUT * BLK, C)
    cell_grad = cell_grad.reshape(SIN * BLK, C)
    return result, cell_grad, grad_in, grad_out, grad_slice


def solution(mesh):
    grid = Mesh(mesh.devices.reshape(4, 2, 8, 4), ("y", "core", "z", "x"))
    whole = ("y", "core", "z", "x")
    placed = (P(whole, None), P(whole), P(whole, None), P(whole, None)) + (P(),) * 9
    return jax.shard_map(
        shards,
        mesh=grid,
        in_specs=placed,
        out_specs=(P(whole, None), P(whole, None), P(), P(), P()),
        check_vma=False,
    )
```

```python
import math

import jax
import jax.numpy as jnp
from jax import lax
from jax.experimental import pallas as pl
from jax.experimental.pallas import tpu as pltpu
from jax.sharding import Mesh, PartitionSpec as P

C = 256
HEADS = 8
SLICES = 64
WIDTH = 32
BLK = 128
SIN = 8
SOUT = 4
GX = 8
GY = 32
PIECE = BLK // GY
ROWS = GY * SOUT * PIECE
HOME = GY * SIN * PIECE
SEND = (SIN + SOUT) * PIECE
GROUP = 4 * SEND
META = 8
TALL = 2 * SEND + META
TOKEN_ROWS = 40
MIX_ROWS = 48
GRAD_ROWS = 56

norm_eps = 1e-05
slice_eps = 1e-05

F32 = jnp.float32
BF16 = jnp.bfloat16
HI = lax.Precision.HIGHEST
NN = (((1,), (0,)), ((), ()))
NT = (((1,), (1,)), ((), ()))
TN = (((0,), (0,)), ((), ()))


def mm(a, b, dims=NN, precision=None):
    return lax.dot_general(a, b, dims, precision=precision, preferred_element_type=F32)


def iota(shape, dim):
    return lax.broadcasted_iota(jnp.int32, shape, dim)


def call(body, outs, *args, scalars=0, hbm=False, hbm_out=(), scratch=(), vmem=40):
    vm = pl.BlockSpec(memory_space=pltpu.VMEM)
    sm = pl.BlockSpec(memory_space=pltpu.SMEM)
    far = pl.BlockSpec(memory_space=pltpu.HBM)
    single = not isinstance(outs, (list, tuple))
    listed = [outs] if single else list(outs)
    moved = sum(math.prod(a.shape) * a.dtype.itemsize for a in list(args) + listed)
    res = pl.pallas_call(
        body,
        out_shape=listed,
        in_specs=[sm] * scalars + [far if hbm else vm] * (len(args) - scalars),
        out_specs=[far if hbm_out is True or i in hbm_out else vm for i in range(len(listed))],
        scratch_shapes=list(scratch),
        compiler_params=pltpu.CompilerParams(vmem_limit_bytes=vmem * 2**20),
        cost_estimate=pl.CostEstimate(flops=0, bytes_accessed=moved, transcendentals=0),
    )(*args)
    return res[0] if single else res


def sds(shape, dtype):
    return jax.ShapeDtypeStruct(shape, dtype)


def column(row):
    n = row.shape[1]
    return jnp.sum(jnp.where(iota((n, n), 0) == iota((n, n), 1), row, 0.0), axis=1, keepdims=True)


def piece_order(back):
    sent = iota((GROUP, GROUP), 1 if back else 0)
    kept = iota((GROUP, GROUP), 0 if back else 1)
    part = (
        (sent >= SEND).astype(jnp.int32)
        + (sent >= 2 * SEND).astype(jnp.int32)
        + (sent >= 3 * SEND).astype(jnp.int32)
    )
    within = sent - part * SEND
    source = (within >> 2) * 16 + part * PIECE + (within & 3)
    return (source == kept).astype(F32).astype(BF16)


def pack_kernel(tally, plan, cells, cot, out, sent, out_sem):
    order = piece_order(False)
    block = iota((META, 128), 1) >> 2
    target = jnp.zeros((META, 128), jnp.int32)
    for s in range(SIN):
        target = jnp.where(block == s, plan[0, s], target)
    held = jnp.clip(tally[0] - block * BLK, 0, BLK)
    meta = jnp.where(iota((META, 128), 0) < 4, target, held).astype(F32).astype(BF16)
    for j in range(GY):
        sent[j, 2 * SEND : TALL, :] = meta
    writes = []
    for j in range(8):
        at = slice(16 * j, 16 * j + 16)
        rows = [cells[:, at, :].reshape(16 * SIN, C), cot[:, at, :].reshape(16 * SOUT, C)]
        moved = mm(order, jnp.concatenate(rows, axis=0)).astype(BF16)
        for a in range(4):
            part = moved[a * SEND : (a + 1) * SEND]
            sent[4 * j + a, 0:SEND, :] = part[:, 0:128]
            sent[4 * j + a, SEND : 2 * SEND, :] = part[:, 128:C]
        group = pl.ds(4 * j, 4)
        copy = pltpu.make_async_copy(sent.at[group], out.at[group], out_sem.at[j])
        copy.start()
        writes.append(copy)
    for copy in writes:
        copy.wait()


def weight_kernel(
    gain, entrance, portion, softness, base, exit_w,
    entrance_t, exit_t, spread_out, soft_spread_out, gain_out, base_out, soft_out,
):
    eye = (iota((C, C), 0) == iota((C, C), 1)).astype(F32).astype(BF16)
    entrance_t[...] = mm(entrance[...], eye, TN).astype(BF16)
    exit_t[...] = mm(exit_w[...], eye, TN).astype(BF16)
    tall = ((iota((C, WIDTH), 0) & 31) == iota((C, WIDTH), 1)).astype(F32).astype(BF16)
    broad = ((iota((SLICES, 512), 1) & 63) == iota((SLICES, 512), 0)).astype(F32).astype(BF16)
    spread = mm(mm(tall, portion[...]).astype(BF16), broad)
    same = (iota((C, 512), 0) >> 5) == (iota((C, 512), 1) >> 6)
    spread_out[...] = jnp.where(same, spread, 0.0).astype(BF16)
    soft_row = mm(softness[...], tall, NT)
    soft_same = (iota((16, C), 1) >> 5) == iota((16, C), 0)
    soft_spread_out[...] = jnp.where(soft_same, soft_row, 0.0).astype(BF16)
    gain_out[...] = jnp.broadcast_to(column(gain[...]), (C, 128))
    base_out[...] = jnp.broadcast_to(column(base[...]), (HEADS, 128))
    soft_out[...] = jnp.broadcast_to(column(softness[...].astype(F32)), (WIDTH, 128))


def forward_kernel(
    spot, recv, entrance_t, exit_w, spread, soft_spread, gain_col, base_col,
    token, pick, xt_out, normed_out, proj_out, prob_out, scaled_out, slice_out,
    uns_out, cot_out, rows_out, heads_out,
):
    mine = spot[0]
    cells = jnp.concatenate(
        [recv[:, a : a + SIN * PIECE, :].reshape(HOME, 128) for a in (0, SEND)], axis=1
    )
    cot = jnp.concatenate(
        [recv[:, a + SIN * PIECE : a + SEND, :].reshape(ROWS, 128) for a in (0, SEND)], axis=1
    )
    meta = recv[:, 2 * SEND : TALL, :].astype(F32)
    upper = iota((GY, META, 128), 1) < 4
    target = jnp.max(jnp.where(upper, meta, -1.0), axis=1)
    held = jnp.max(jnp.where(upper, 0.0, meta), axis=1)

    lane = iota((GY, 128), 1)
    lane_f = lane.astype(F32)
    hits = [(target[:, 4 * s : 4 * s + 1] == lane_f).astype(F32) for s in range(SIN)]
    taken = hits[0]
    for s in range(1, SIN):
        taken = taken + hits[s]
    before = (iota((GY, GY), 1) < iota((GY, GY), 0)).astype(F32).astype(BF16)
    place = mm(before, taken.astype(BF16)) + lane_f * SOUT + 1.0
    dest = jnp.zeros((GY, 128), F32)
    for s in range(SIN):
        found = jnp.sum(hits[s] * place, axis=1, keepdims=True)
        dest = jnp.where((lane >> 2) == s, found, dest)
    row_in_block = (mine * PIECE + (lane & 3)).astype(F32)
    dest = jnp.where(row_in_block < held, dest, 0.0) - 1.0
    flip = (iota((128, 128), 0) == iota((128, 128), 1)).astype(F32).astype(BF16)
    slots = mm(flip, dest.astype(BF16), NT)[0:32, :]
    slots = (slots * 4.0 + (iota((32, GY), 0) & 3).astype(F32)).astype(jnp.int32)
    at_row = iota((32, ROWS), 1)
    seen = jnp.zeros((32, ROWS), F32)
    for p in range(GY):
        match = (slots[:, p : p + 1] == at_row).astype(F32)
        seen = seen + match
        pick[p * 32 : (p + 1) * 32, :] = match.astype(BF16)
    live = jnp.sum(seen, axis=0, keepdims=True)

    xt = mm(cells, pick[...], TN)
    xt_out[...] = xt.astype(BF16)
    mean = jnp.sum(xt, axis=0, keepdims=True) * (1.0 / C)
    centered = xt - mean
    var = jnp.sum(centered * centered, axis=0, keepdims=True) * (1.0 / C)
    inv = lax.rsqrt(var + norm_eps)
    normed = (centered * inv * gain_col[:, 0:1]).astype(BF16)
    normed_out[...] = normed
    proj_out[...] = mm(entrance_t[...], normed).astype(BF16)
    rows_out[0:1, :] = live
    rows_out[1:2, :] = mean
    rows_out[2:3, :] = inv

    mid = proj_out[C : 2 * C, :]
    presq = mm(soft_spread[...], mid)[0:HEADS]
    softplus = jnp.maximum(presq, 0.0) + jnp.log1p(jnp.exp(-jnp.abs(presq)))
    inv_temp = 1.0 / (base_col[:, 0:1] + softplus)
    heads_out[0:8, :] = inv_temp
    heads_out[8:16, :] = presq
    scaled_out[...] = mm(spread[...], mid, TN)

    back = mm(exit_w[...], cot, NT) * live
    uns_out[...] = back.astype(BF16)
    eye = (iota((C, C), 0) == iota((C, C), 1)).astype(F32).astype(BF16)
    cot_out[...] = (mm(eye, cot, NT) * live).astype(BF16)

    for h in range(HEADS):
        at = h * SLICES
        scaled = scaled_out[at : at + SLICES, :] * inv_temp[h : h + 1, :]
        scaled_out[at : at + SLICES, :] = scaled
        top = jnp.max(scaled, axis=0, keepdims=True)
        e = jnp.exp(scaled - top)
        prob = e * (1.0 / jnp.sum(e, axis=0, keepdims=True))
        prob_out[at : at + SLICES, :] = prob
        half = (prob * live).astype(BF16)
        slice_out[at : at + SLICES, :] = half
        left = jnp.concatenate(
            [
                proj_out[h * WIDTH : (h + 1) * WIDTH, :],
                uns_out[h * WIDTH : (h + 1) * WIDTH, :],
                jnp.ones((16, ROWS), BF16),
            ],
            axis=0,
        )
        sums = mm(left, half, NT)
        main = jnp.concatenate([sums[0:WIDTH], sums[WIDTH : 2 * WIDTH]], axis=1)
        count = jnp.concatenate([sums[2 * WIDTH : 2 * WIDTH + 8]] * 2, axis=1)
        token[h] = jnp.concatenate([main, count], axis=0).astype(BF16)


def spread_kernel(recv, out):
    n = recv.shape[0]
    total = recv[0].astype(F32)
    for i in range(1, n):
        total = total + recv[i].astype(F32)
    total = total.astype(out.dtype)
    for i in range(out.shape[0]):
        out[i] = total


def spread_sum(recv, copies, dtype):
    return call(spread_kernel, sds((copies,) + recv.shape[1:], dtype), recv)


def token_kernel(recv, request, lookup, content, out):
    total = recv[0].astype(F32)
    for i in range(1, GY):
        total = total + recv[i].astype(F32)
    inverse = 1.0 / (total[WIDTH : WIDTH + 1, 0:SLICES] + slice_eps)
    tok = total[0:WIDTH, 0:SLICES] * inverse
    cot = total[0:WIDTH, SLICES:128]
    scale = WIDTH ** (-0.5)
    joined = jnp.concatenate([request[...], lookup[...], content[...]], axis=1)
    qkv = mm(joined, tok, TN, HI)
    q, k, v = (qkv[i * WIDTH : (i + 1) * WIDTH] for i in range(3))
    scores = mm(k, q, TN, HI) * scale
    e = jnp.exp(scores - jnp.max(scores, axis=0, keepdims=True))
    att = e / jnp.sum(e, axis=0, keepdims=True)
    mixed = mm(v, att, NN, HI)
    g_att = mm(v, cot, TN, HI)
    g_v = mm(cot, att, NT, HI)
    g_s = att * (g_att - jnp.sum(att * g_att, axis=0, keepdims=True)) * scale
    g_q = mm(k, g_s, NN, HI)
    g_k = mm(q, g_s, NT, HI)
    g_tok = mm(joined, jnp.concatenate([g_q, g_k, g_v], axis=0), NN, HI)
    g_num = g_tok * inverse
    g_den = -jnp.sum(g_tok * tok, axis=0, keepdims=True) * inverse
    g_den_hi = g_den.astype(BF16).astype(F32)
    g_den_lo = g_den - g_den_hi
    main = jnp.concatenate([mixed, g_num], axis=1).astype(BF16)
    tail = jnp.concatenate([g_den_hi, g_den_lo], axis=1)
    tail = jnp.broadcast_to(tail, (16, 128)).astype(BF16)
    for i in range(GX):
        out[i, 0:WIDTH, :] = main
        out[i, WIDTH:MIX_ROWS, :] = tail


def backward_kernel(
    mix, spread, soft_col, normed_in, proj_in, prob_in, scaled_in, slice_in,
    uns_in, cot_in, rows_in, heads_in,
    grads_out, gproj, deslice_out, weave, stack, gprob, affs, grads, sem,
):
    live = rows_in[0:1, :]
    weave[...] = jnp.zeros_like(weave)
    lane = iota((WIDTH, 128), 1)
    lane16 = iota((16, 128), 1)
    sub16 = iota((16, 128), 0)
    for h in range(HEADS):
        block = mix[h].astype(F32)
        turned = pltpu.roll(block, SLICES, 1)
        low = h % 2 == 0
        left, right = (block, turned) if low else (turned, block)
        here = (lane < SLICES) if low else (lane >= SLICES)
        at = (h // 2) * 128
        weave[h * WIDTH : (h + 1) * WIDTH, at : at + 128] = jnp.where(
            here, left[0:WIDTH], 0.0
        ).astype(BF16)
        weave[C + h * WIDTH : C + (h + 1) * WIDTH, at : at + 128] = jnp.where(
            here, right[0:WIDTH], 0.0
        ).astype(BF16)
    for g in range(HEADS // 2):
        even = mix[2 * g, WIDTH:MIX_ROWS, :].astype(F32)
        odd = mix[2 * g + 1, WIDTH:MIX_ROWS, :].astype(F32)
        upper = jnp.where(lane16 < SLICES, even, pltpu.roll(odd, SLICES, 1))
        lower = jnp.where(lane16 < SLICES, pltpu.roll(even, SLICES, 1), odd)
        both = jnp.where(sub16 == 0, upper, jnp.where(sub16 == 1, lower, 0.0))
        weave[2 * C : 2 * C + 16, g * 128 : (g + 1) * 128] = both.astype(BF16)
    stack[0:C, :] = uns_in[...]
    stack[C : 2 * C, :] = proj_in[0:C, :]
    stack[2 * C : 2 * C + 16, :] = jnp.ones((16, ROWS), BF16)

    rows = mm(weave[0 : 2 * C, :], slice_in[...])
    deslice = rows[0:C].astype(BF16)
    gproj[0:C, :] = rows[C : 2 * C].astype(BF16)
    gprob[...] = mm(weave[...], stack[...], TN)
    deslice_out[...] = deslice
    out_grad = mm(deslice, cot_in[...], NT)
    for b in range(2):
        grads[(4 + b) * C : (5 + b) * C, :] = out_grad[:, b * 128 : (b + 1) * 128].astype(
            grads.dtype
        )

    copies = []

    def write(first, last):
        span = pl.ds(first, last - first)
        copy = pltpu.make_async_copy(grads.at[span], grads_out.at[span], sem.at[len(copies)])
        copy.start()
        copies.append(copy)

    def write_half(half):
        in_grad = mm(normed_in[...], gproj[half * C : (half + 1) * C, :], NT)
        for b in range(2):
            at = (2 * half + b) * C
            grads[at : at + C, :] = in_grad[:, b * 128 : (b + 1) * 128].astype(grads.dtype)
        write(2 * half * C, 2 * (half + 1) * C)

    write(4 * C, 6 * C)
    write_half(0)
    softs = []
    for h in range(HEADS):
        at = h * SLICES
        inv_temp = heads_in[h : h + 1, :]
        presq = heads_in[8 + h : 9 + h, :]
        prob = prob_in[at : at + SLICES, :]
        gp = gprob[at : at + SLICES, :] * live
        adj = prob * (gp - jnp.sum(prob * gp, axis=0, keepdims=True))
        affs[at : at + SLICES, :] = (adj * inv_temp).astype(BF16)
        pulled = jnp.sum(adj * scaled_in[at : at + SLICES, :], axis=0, keepdims=True)
        softs.append(-pulled * inv_temp * (1.0 / (1.0 + jnp.exp(-presq))))
    between = mm(spread[...], affs[...])
    slice_grad = jnp.zeros((WIDTH, SLICES), F32)
    for h in range(HEADS):
        at = h * WIDTH
        part = between[at : at + WIDTH] + soft_col[:, 0:1] * softs[h]
        gproj[C + at : C + at + WIDTH, :] = part.astype(BF16)
        slice_grad = slice_grad + mm(
            proj_in[C + at : C + at + WIDTH, :], affs[h * SLICES : (h + 1) * SLICES, :], NT
        )
    write_half(1)
    tail = jnp.concatenate([slice_grad, jnp.zeros((WIDTH, SLICES), F32)], axis=1)
    grads[6 * C : 6 * C + WIDTH, :] = tail.astype(grads.dtype)
    grads[6 * C + WIDTH :, :] = jnp.zeros((GY * GRAD_ROWS - 6 * C - WIDTH, 128), grads.dtype)
    write(6 * C, GY * GRAD_ROWS)
    for copy in copies:
        copy.wait()


def home_kernel(
    entrance, exit_t, gain_col, pick, xt_in, cot_in, rows_in, gproj, deslice, send
):
    live = rows_in[0:1, :]
    mean = rows_in[1:2, :]
    inv = rows_in[2:3, :]
    xt = xt_in[...].astype(F32)
    result = (live * (xt + mm(exit_t[...], deslice[...]))).astype(BF16)
    eye = (iota((ROWS, ROWS), 0) == iota((ROWS, ROWS), 1)).astype(F32).astype(BF16)
    result_rows = mm(eye, result, NT).astype(BF16)
    for q in range(GY):
        send[q, SIN * PIECE : SEND, :] = result_rows[q * 16 : (q + 1) * 16]
    g_unit = mm(entrance[...], gproj[...]) * gain_col[:, 0:1]
    unit = (xt - mean) * inv
    m1 = jnp.sum(g_unit, axis=0, keepdims=True) * (1.0 / C)
    m2 = jnp.sum(g_unit * unit, axis=0, keepdims=True) * (1.0 / C)
    cell = cot_in[...].astype(F32) + inv * (g_unit - m1 - unit * m2)
    cell_rows = mm(pick[...], cell.astype(BF16), NT).astype(BF16)
    for q in range(GY):
        send[q, 0 : SIN * PIECE, :] = cell_rows[q * 32 : (q + 1) * 32]


def gather_kernel(
    scale, at, r0, r1, grad_in, grad_out, grad_slice, flat, tail, sem
):
    y, core, x = at[0], at[1], at[2]
    for dc, recv in enumerate((r0, r1)):
        for dy in range(4):
            for dx in range(4):
                index = (((y - dy) & 3) * 2 + (core ^ dc)) * 4 + ((x - dx) & 3)
                start = pl.multiple_of(index * GRAD_ROWS, 8)
                flat[pl.ds(start, GRAD_ROWS), :] = recv[dy * 4 + dx].astype(F32) * scale
    tail[...] = flat[6 * C : 6 * C + WIDTH, 0:SLICES]
    copies = []
    for b in range(6):
        out, c = (grad_in, b) if b < 4 else (grad_out, b - 4)
        target = out.at[:, c * 128 : (c + 1) * 128]
        copies.append(pltpu.make_async_copy(flat.at[b * C : (b + 1) * C], target, sem.at[b]))
    copies.append(pltpu.make_async_copy(tail, grad_slice, sem.at[6]))
    for copy in copies:
        copy.start()
    for copy in copies:
        copy.wait()


def unpack_kernel(home, result, cell_grad, cells, rows, sem):
    copies = []
    order = piece_order(True)
    for j in range(8):
        got = jnp.concatenate([home[4 * j + a] for a in range(4)], axis=0)
        moved = mm(order, got).astype(BF16)
        span = pl.ds(16 * j, 16)
        cells[:, span, :] = moved[0 : SIN * 16].reshape(SIN, 16, C)
        rows[:, span, :] = moved[SIN * 16 :].reshape(SOUT, 16, C)
        if j % 2 == 1:
            both = pl.ds(16 * (j - 1), 32)
            pair = [
                pltpu.make_async_copy(cells.at[:, both, :], cell_grad.at[:, both, :], sem.at[j - 1]),
                pltpu.make_async_copy(rows.at[:, both, :], result.at[:, both, :], sem.at[j]),
            ]
            for copy in pair:
                copy.start()
            copies += pair
    for copy in copies:
        copy.wait()


def shards(
    cells, tally, plan, cot, gain, entrance, portion, softness, base,
    request, lookup, content, exit_w,
):
    gain = gain.reshape(1, C)
    softness = softness.reshape(1, WIDTH)
    base = base.reshape(1, HEADS)
    scale = 1.0 / math.sqrt(GX * GY * SIN * BLK)

    def swap(x, axes):
        return lax.all_to_all(x, axes, 0, 0, tiled=True)

    def shifted(x, axis, n, d):
        return lax.ppermute(x, axis, [(i, (i + d) % n) for i in range(n)])

    sent = call(
        pack_kernel,
        sds((GY, TALL, 128), BF16),
        tally, plan, cells.reshape(SIN, BLK, C), cot.reshape(SOUT, BLK, C),
        scalars=2,
        hbm_out=True,
        vmem=62,
        scratch=[
            pltpu.VMEM((GY, TALL, 128), BF16),
            pltpu.SemaphoreType.DMA((8,)),
        ],
    )
    entrance_t, exit_t, spread, soft_spread, gain_col, base_col, soft_col = call(
        weight_kernel,
        [
            sds((2 * C, C), BF16),
            sds((C, C), BF16),
            sds((C, 512), BF16),
            sds((16, C), BF16),
            sds((C, 128), F32),
            sds((HEADS, 128), F32),
            sds((WIDTH, 128), F32),
        ],
        gain, entrance, portion, softness, base, exit_w,
    )
    recv = swap(sent, ("z", "x"))
    spot = (lax.axis_index("z") * 4 + lax.axis_index("x")).astype(jnp.int32).reshape(1)
    state = call(
        forward_kernel,
        [
            sds((HEADS, TOKEN_ROWS, 128), BF16),
            sds((HOME, ROWS), BF16),
            sds((C, ROWS), BF16),
            sds((C, ROWS), BF16),
            sds((2 * C, ROWS), BF16),
            sds((512, ROWS), F32),
            sds((512, ROWS), F32),
            sds((512, ROWS), BF16),
            sds((C, ROWS), BF16),
            sds((C, ROWS), BF16),
            sds((8, ROWS), F32),
            sds((16, ROWS), F32),
        ],
        spot, recv, entrance_t, exit_w, spread, soft_spread, gain_col, base_col,
        scalars=1,
    )
    token, pick, xt, normed, proj, prob, scaled, slices, uns, cot_t, rows, heads = state
    token = swap(token, ("y", "core"))
    token = swap(spread_sum(token, GY, BF16), ("z", "x"))
    mix = call(
        token_kernel, sds((GX, MIX_ROWS, 128), BF16), token, request, lookup, content
    )
    mix = swap(mix, ("y", "core"))
    grads, gproj, deslice = call(
        backward_kernel,
        [
            sds((GY * GRAD_ROWS, 128), BF16),
            sds((2 * C, ROWS), BF16),
            sds((C, ROWS), BF16),
        ],
        mix, spread, soft_col, normed, proj, prob, scaled, slices, uns, cot_t, rows, heads,
        scratch=[
            pltpu.VMEM((2 * C + 16, 512), BF16),
            pltpu.VMEM((2 * C + 16, ROWS), BF16),
            pltpu.VMEM((512, ROWS), F32),
            pltpu.VMEM((512, ROWS), BF16),
            pltpu.VMEM((GY * GRAD_ROWS, 128), BF16),
            pltpu.SemaphoreType.DMA((4,)),
        ],
        hbm_out=(0,),
    )
    send = call(
        home_kernel,
        sds((GY, SEND, C), BF16),
        entrance, exit_t, gain_col, pick, xt, cot_t, rows, gproj, deslice,
    )
    grads = swap(grads.reshape(GY, GRAD_ROWS, 128), ("y", "core", "x"))
    grads = spread_sum(grads, 8, BF16)
    send, grads = lax.optimization_barrier((send, grads))
    grads = swap(grads, ("z",))
    grads = spread_sum(grads, 1, BF16)
    send, grads = lax.optimization_barrier((send, grads))
    home = swap(send, ("z", "x"))
    for axis in ("x", "y"):
        grads = jnp.concatenate([grads] + [shifted(grads, axis, 4, d) for d in (1, 2, 3)], axis=0)
    gathered = [grads, shifted(grads, "core", 2, 1)]
    at = jnp.stack([lax.axis_index(a) for a in ("y", "core", "x")]).astype(jnp.int32)
    result, cell_grad = call(
        unpack_kernel,
        [sds((SOUT, BLK, C), BF16), sds((SIN, BLK, C), BF16)],
        home,
        hbm_out=True,
        scratch=[
            pltpu.VMEM((SIN, BLK, C), BF16),
            pltpu.VMEM((SOUT, BLK, C), BF16),
            pltpu.SemaphoreType.DMA((8,)),
        ],
    )
    grad_in, grad_out, grad_slice = call(
        lambda *refs: gather_kernel(scale, *refs),
        [sds((C, 2 * C), F32), sds((C, C), F32), sds((WIDTH, SLICES), F32)],
        at, *gathered,
        scalars=1,
        hbm_out=True,
        scratch=[
            pltpu.VMEM((GY * GRAD_ROWS, 128), F32),
            pltpu.VMEM((WIDTH, SLICES), F32),
            pltpu.SemaphoreType.DMA((7,)),
        ],
    )
    result = result.reshape(SOUT * BLK, C)
    cell_grad = cell_grad.reshape(SIN * BLK, C)
    return result, cell_grad, grad_in, grad_out, grad_slice


def solution(mesh):
    grid = Mesh(mesh.devices.reshape(4, 2, 8, 4), ("y", "core", "z", "x"))
    whole = ("y", "core", "z", "x")
    placed = (P(whole, None), P(whole), P(whole, None), P(whole, None)) + (P(),) * 9
    return jax.shard_map(
        shards,
        mesh=grid,
        in_specs=placed,
        out_specs=(P(whole, None), P(whole, None), P(), P(), P()),
        check_vma=False,
    )
```

```python
import math

import jax
import jax.numpy as jnp
from jax import lax
from jax.experimental import pallas as pl
from jax.experimental.pallas import tpu as pltpu
from jax.sharding import Mesh, PartitionSpec as P

C = 256
HEADS = 8
SLICES = 64
WIDTH = 32
BLK = 128
SIN = 8
SOUT = 4
GX = 8
GY = 32
PIECE = BLK // GY
ROWS = GY * SOUT * PIECE
HOME = GY * SIN * PIECE
SEND = (SIN + SOUT) * PIECE
GROUP = 4 * SEND
META = 8
TALL = 2 * SEND + META
TOKEN_ROWS = 40
MIX_ROWS = 48
GRAD_ROWS = 56

norm_eps = 1e-05
slice_eps = 1e-05

F32 = jnp.float32
BF16 = jnp.bfloat16
HI = lax.Precision.HIGHEST
NN = (((1,), (0,)), ((), ()))
NT = (((1,), (1,)), ((), ()))
TN = (((0,), (0,)), ((), ()))


def mm(a, b, dims=NN, precision=None):
    return lax.dot_general(a, b, dims, precision=precision, preferred_element_type=F32)


def iota(shape, dim):
    return lax.broadcasted_iota(jnp.int32, shape, dim)


def call(body, outs, *args, scalars=0, hbm=False, hbm_out=False, scratch=(), vmem=40):
    vm = pl.BlockSpec(memory_space=pltpu.VMEM)
    sm = pl.BlockSpec(memory_space=pltpu.SMEM)
    far = pl.BlockSpec(memory_space=pltpu.HBM)
    single = not isinstance(outs, (list, tuple))
    listed = [outs] if single else list(outs)
    moved = sum(math.prod(a.shape) * a.dtype.itemsize for a in list(args) + listed)
    res = pl.pallas_call(
        body,
        out_shape=listed,
        in_specs=[sm] * scalars + [far if hbm else vm] * (len(args) - scalars),
        out_specs=[far if hbm_out else vm] * len(listed),
        scratch_shapes=list(scratch),
        compiler_params=pltpu.CompilerParams(vmem_limit_bytes=vmem * 2**20),
        cost_estimate=pl.CostEstimate(flops=0, bytes_accessed=moved, transcendentals=0),
    )(*args)
    return res[0] if single else res


def sds(shape, dtype):
    return jax.ShapeDtypeStruct(shape, dtype)


def column(row):
    n = row.shape[1]
    return jnp.sum(jnp.where(iota((n, n), 0) == iota((n, n), 1), row, 0.0), axis=1, keepdims=True)


def piece_order(back):
    sent = iota((GROUP, GROUP), 1 if back else 0)
    kept = iota((GROUP, GROUP), 0 if back else 1)
    part = (
        (sent >= SEND).astype(jnp.int32)
        + (sent >= 2 * SEND).astype(jnp.int32)
        + (sent >= 3 * SEND).astype(jnp.int32)
    )
    within = sent - part * SEND
    source = (within >> 2) * 16 + part * PIECE + (within & 3)
    return (source == kept).astype(F32).astype(BF16)


def pack_kernel(tally, plan, cells, cot, out, sent, out_sem):
    order = piece_order(False)
    block = iota((META, 128), 1) >> 2
    target = jnp.zeros((META, 128), jnp.int32)
    for s in range(SIN):
        target = jnp.where(block == s, plan[0, s], target)
    held = jnp.clip(tally[0] - block * BLK, 0, BLK)
    meta = jnp.where(iota((META, 128), 0) < 4, target, held).astype(F32).astype(BF16)
    for j in range(GY):
        sent[j, 2 * SEND : TALL, :] = meta
    writes = []
    for j in range(8):
        at = slice(16 * j, 16 * j + 16)
        rows = [cells[:, at, :].reshape(16 * SIN, C), cot[:, at, :].reshape(16 * SOUT, C)]
        moved = mm(order, jnp.concatenate(rows, axis=0)).astype(BF16)
        for a in range(4):
            part = moved[a * SEND : (a + 1) * SEND]
            sent[4 * j + a, 0:SEND, :] = part[:, 0:128]
            sent[4 * j + a, SEND : 2 * SEND, :] = part[:, 128:C]
        group = pl.ds(4 * j, 4)
        copy = pltpu.make_async_copy(sent.at[group], out.at[group], out_sem.at[j])
        copy.start()
        writes.append(copy)
    for copy in writes:
        copy.wait()


def weight_kernel(
    gain, entrance, portion, softness, base, exit_w,
    entrance_t, exit_t, spread_out, soft_spread_out, gain_out, base_out, soft_out,
):
    eye = (iota((C, C), 0) == iota((C, C), 1)).astype(F32).astype(BF16)
    entrance_t[...] = mm(entrance[...], eye, TN).astype(BF16)
    exit_t[...] = mm(exit_w[...], eye, TN).astype(BF16)
    tall = ((iota((C, WIDTH), 0) & 31) == iota((C, WIDTH), 1)).astype(F32).astype(BF16)
    broad = ((iota((SLICES, 512), 1) & 63) == iota((SLICES, 512), 0)).astype(F32).astype(BF16)
    spread = mm(mm(tall, portion[...]).astype(BF16), broad)
    same = (iota((C, 512), 0) >> 5) == (iota((C, 512), 1) >> 6)
    spread_out[...] = jnp.where(same, spread, 0.0).astype(BF16)
    soft_row = mm(softness[...], tall, NT)
    soft_same = (iota((16, C), 1) >> 5) == iota((16, C), 0)
    soft_spread_out[...] = jnp.where(soft_same, soft_row, 0.0).astype(BF16)
    gain_out[...] = jnp.broadcast_to(column(gain[...]), (C, 128))
    base_out[...] = jnp.broadcast_to(column(base[...]), (HEADS, 128))
    soft_out[...] = jnp.broadcast_to(column(softness[...].astype(F32)), (WIDTH, 128))


def forward_kernel(
    spot, recv, entrance_t, exit_w, spread, soft_spread, gain_col, base_col,
    token, pick, xt_out, normed_out, proj_out, prob_out, scaled_out, slice_out,
    uns_out, cot_out, rows_out, heads_out,
):
    mine = spot[0]
    cells = jnp.concatenate(
        [recv[:, a : a + SIN * PIECE, :].reshape(HOME, 128) for a in (0, SEND)], axis=1
    )
    cot = jnp.concatenate(
        [recv[:, a + SIN * PIECE : a + SEND, :].reshape(ROWS, 128) for a in (0, SEND)], axis=1
    )
    meta = recv[:, 2 * SEND : TALL, :].astype(F32)
    upper = iota((GY, META, 128), 1) < 4
    target = jnp.max(jnp.where(upper, meta, -1.0), axis=1)
    held = jnp.max(jnp.where(upper, 0.0, meta), axis=1)

    lane = iota((GY, 128), 1)
    lane_f = lane.astype(F32)
    hits = [(target[:, 4 * s : 4 * s + 1] == lane_f).astype(F32) for s in range(SIN)]
    taken = hits[0]
    for s in range(1, SIN):
        taken = taken + hits[s]
    before = (iota((GY, GY), 1) < iota((GY, GY), 0)).astype(F32).astype(BF16)
    place = mm(before, taken.astype(BF16)) + lane_f * SOUT + 1.0
    dest = jnp.zeros((GY, 128), F32)
    for s in range(SIN):
        found = jnp.sum(hits[s] * place, axis=1, keepdims=True)
        dest = jnp.where((lane >> 2) == s, found, dest)
    row_in_block = (mine * PIECE + (lane & 3)).astype(F32)
    dest = jnp.where(row_in_block < held, dest, 0.0) - 1.0
    flip = (iota((128, 128), 0) == iota((128, 128), 1)).astype(F32).astype(BF16)
    slots = mm(flip, dest.astype(BF16), NT)[0:32, :]
    slots = (slots * 4.0 + (iota((32, GY), 0) & 3).astype(F32)).astype(jnp.int32)
    at_row = iota((32, ROWS), 1)
    seen = jnp.zeros((32, ROWS), F32)
    for p in range(GY):
        match = (slots[:, p : p + 1] == at_row).astype(F32)
        seen = seen + match
        pick[p * 32 : (p + 1) * 32, :] = match.astype(BF16)
    live = jnp.sum(seen, axis=0, keepdims=True)

    xt = mm(cells, pick[...], TN)
    xt_out[...] = xt.astype(BF16)
    mean = jnp.sum(xt, axis=0, keepdims=True) * (1.0 / C)
    centered = xt - mean
    var = jnp.sum(centered * centered, axis=0, keepdims=True) * (1.0 / C)
    inv = lax.rsqrt(var + norm_eps)
    normed = (centered * inv * gain_col[:, 0:1]).astype(BF16)
    normed_out[...] = normed
    proj_out[...] = mm(entrance_t[...], normed).astype(BF16)
    rows_out[0:1, :] = live
    rows_out[1:2, :] = mean
    rows_out[2:3, :] = inv

    mid = proj_out[C : 2 * C, :]
    presq = mm(soft_spread[...], mid)[0:HEADS]
    softplus = jnp.maximum(presq, 0.0) + jnp.log1p(jnp.exp(-jnp.abs(presq)))
    inv_temp = 1.0 / (base_col[:, 0:1] + softplus)
    heads_out[0:8, :] = inv_temp
    heads_out[8:16, :] = presq
    scaled_out[...] = mm(spread[...], mid, TN)

    back = mm(exit_w[...], cot, NT) * live
    uns_out[...] = back.astype(BF16)
    eye = (iota((C, C), 0) == iota((C, C), 1)).astype(F32).astype(BF16)
    cot_out[...] = (mm(eye, cot, NT) * live).astype(BF16)

    for h in range(HEADS):
        at = h * SLICES
        scaled = scaled_out[at : at + SLICES, :] * inv_temp[h : h + 1, :]
        scaled_out[at : at + SLICES, :] = scaled
        top = jnp.max(scaled, axis=0, keepdims=True)
        e = jnp.exp(scaled - top)
        prob = e * (1.0 / jnp.sum(e, axis=0, keepdims=True))
        prob_out[at : at + SLICES, :] = prob
        half = (prob * live).astype(BF16)
        slice_out[at : at + SLICES, :] = half
        left = jnp.concatenate(
            [
                proj_out[h * WIDTH : (h + 1) * WIDTH, :],
                uns_out[h * WIDTH : (h + 1) * WIDTH, :],
                jnp.ones((16, ROWS), BF16),
            ],
            axis=0,
        )
        sums = mm(left, half, NT)
        main = jnp.concatenate([sums[0:WIDTH], sums[WIDTH : 2 * WIDTH]], axis=1)
        count = jnp.concatenate([sums[2 * WIDTH : 2 * WIDTH + 8]] * 2, axis=1)
        token[h] = jnp.concatenate([main, count], axis=0).astype(BF16)


def spread_kernel(recv, out):
    n = recv.shape[0]
    total = recv[0].astype(F32)
    for i in range(1, n):
        total = total + recv[i].astype(F32)
    total = total.astype(out.dtype)
    for i in range(out.shape[0]):
        out[i] = total


def spread_sum(recv, copies, dtype):
    return call(spread_kernel, sds((copies,) + recv.shape[1:], dtype), recv)


def token_kernel(recv, request, lookup, content, out):
    total = recv[0].astype(F32)
    for i in range(1, GY):
        total = total + recv[i].astype(F32)
    inverse = 1.0 / (total[WIDTH : WIDTH + 1, 0:SLICES] + slice_eps)
    tok = total[0:WIDTH, 0:SLICES] * inverse
    cot = total[0:WIDTH, SLICES:128]
    scale = WIDTH ** (-0.5)
    q = mm(request[...], tok, TN, HI)
    k = mm(lookup[...], tok, TN, HI)
    v = mm(content[...], tok, TN, HI)
    scores = mm(k, q, TN, HI) * scale
    e = jnp.exp(scores - jnp.max(scores, axis=0, keepdims=True))
    att = e / jnp.sum(e, axis=0, keepdims=True)
    mixed = mm(v, att, NN, HI)
    g_att = mm(v, cot, TN, HI)
    g_v = mm(cot, att, NT, HI)
    g_s = att * (g_att - jnp.sum(att * g_att, axis=0, keepdims=True)) * scale
    g_q = mm(k, g_s, NN, HI)
    g_k = mm(q, g_s, NT, HI)
    g_tok = mm(request[...], g_q, NN, HI)
    g_tok = g_tok + mm(lookup[...], g_k, NN, HI)
    g_tok = g_tok + mm(content[...], g_v, NN, HI)
    g_num = g_tok * inverse
    g_den = -jnp.sum(g_tok * tok, axis=0, keepdims=True) * inverse
    g_den_hi = g_den.astype(BF16).astype(F32)
    g_den_lo = g_den - g_den_hi
    main = jnp.concatenate([mixed, g_num], axis=1).astype(BF16)
    tail = jnp.concatenate([g_den_hi, g_den_lo], axis=1)
    tail = jnp.broadcast_to(tail, (16, 128)).astype(BF16)
    for i in range(GX):
        out[i, 0:WIDTH, :] = main
        out[i, WIDTH:MIX_ROWS, :] = tail


def backward_kernel(
    mix, entrance, exit_t, spread, gain_col, soft_col,
    pick, xt_in, normed_in, proj_in, prob_in, scaled_in, slice_in,
    uns_in, cot_in, rows_in, heads_in,
    send, grads, weave, stack, gprob, affs, gproj,
):
    live = rows_in[0:1, :]
    mean = rows_in[1:2, :]
    inv = rows_in[2:3, :]
    weave[...] = jnp.zeros_like(weave)
    lane = iota((WIDTH, 128), 1)
    lane16 = iota((16, 128), 1)
    sub16 = iota((16, 128), 0)
    for h in range(HEADS):
        block = mix[h].astype(F32)
        turned = pltpu.roll(block, SLICES, 1)
        low = h % 2 == 0
        left, right = (block, turned) if low else (turned, block)
        here = (lane < SLICES) if low else (lane >= SLICES)
        at = (h // 2) * 128
        weave[h * WIDTH : (h + 1) * WIDTH, at : at + 128] = jnp.where(
            here, left[0:WIDTH], 0.0
        ).astype(BF16)
        weave[C + h * WIDTH : C + (h + 1) * WIDTH, at : at + 128] = jnp.where(
            here, right[0:WIDTH], 0.0
        ).astype(BF16)
    for g in range(HEADS // 2):
        even = mix[2 * g, WIDTH:MIX_ROWS, :].astype(F32)
        odd = mix[2 * g + 1, WIDTH:MIX_ROWS, :].astype(F32)
        upper = jnp.where(lane16 < SLICES, even, pltpu.roll(odd, SLICES, 1))
        lower = jnp.where(lane16 < SLICES, pltpu.roll(even, SLICES, 1), odd)
        both = jnp.where(sub16 == 0, upper, jnp.where(sub16 == 1, lower, 0.0))
        weave[2 * C : 2 * C + 16, g * 128 : (g + 1) * 128] = both.astype(BF16)
    stack[0:C, :] = uns_in[...]
    stack[C : 2 * C, :] = proj_in[0:C, :]
    stack[2 * C : 2 * C + 16, :] = jnp.ones((16, ROWS), BF16)

    rows = mm(weave[0 : 2 * C, :], slice_in[...])
    deslice = rows[0:C].astype(BF16)
    gproj[0:C, :] = rows[C : 2 * C].astype(BF16)
    gprob[...] = mm(weave[...], stack[...], TN)
    branch = mm(exit_t[...], deslice)
    xt = xt_in[...].astype(F32)
    result = (live * (xt + branch)).astype(BF16)
    eye = (iota((ROWS, ROWS), 0) == iota((ROWS, ROWS), 1)).astype(F32).astype(BF16)
    result_rows = mm(eye, result, NT).astype(BF16)
    for q in range(GY):
        send[q, SIN * PIECE : SEND, :] = result_rows[q * 16 : (q + 1) * 16]
    out_grad = mm(deslice, cot_in[...], NT)
    for b in range(2):
        grads[(4 + b) * C : (5 + b) * C, :] = out_grad[:, b * 128 : (b + 1) * 128].astype(
            grads.dtype
        )

    softs = []
    for h in range(HEADS):
        at = h * SLICES
        inv_temp = heads_in[h : h + 1, :]
        presq = heads_in[8 + h : 9 + h, :]
        prob = prob_in[at : at + SLICES, :]
        gp = gprob[at : at + SLICES, :] * live
        adj = prob * (gp - jnp.sum(prob * gp, axis=0, keepdims=True))
        affs[at : at + SLICES, :] = (adj * inv_temp).astype(BF16)
        pulled = jnp.sum(adj * scaled_in[at : at + SLICES, :], axis=0, keepdims=True)
        softs.append(-pulled * inv_temp * (1.0 / (1.0 + jnp.exp(-presq))))
    between = mm(spread[...], affs[...])
    slice_grad = jnp.zeros((WIDTH, SLICES), F32)
    for h in range(HEADS):
        at = h * WIDTH
        part = between[at : at + WIDTH] + soft_col[:, 0:1] * softs[h]
        gproj[C + at : C + at + WIDTH, :] = part.astype(BF16)
        slice_grad = slice_grad + mm(
            proj_in[C + at : C + at + WIDTH, :], affs[h * SLICES : (h + 1) * SLICES, :], NT
        )
    in_grad = mm(normed_in[...], gproj[...], NT)
    for b in range(4):
        grads[b * C : (b + 1) * C, :] = in_grad[:, b * 128 : (b + 1) * 128].astype(grads.dtype)
    tail = jnp.concatenate([slice_grad, jnp.zeros((WIDTH, SLICES), F32)], axis=1)
    grads[6 * C : 6 * C + WIDTH, :] = tail.astype(grads.dtype)
    grads[6 * C + WIDTH :, :] = jnp.zeros((GY * GRAD_ROWS - 6 * C - WIDTH, 128), grads.dtype)

    g_unit = mm(entrance[...], gproj[...]) * gain_col[:, 0:1]
    unit = (xt - mean) * inv
    m1 = jnp.sum(g_unit, axis=0, keepdims=True) * (1.0 / C)
    m2 = jnp.sum(g_unit * unit, axis=0, keepdims=True) * (1.0 / C)
    cell = cot_in[...].astype(F32) + inv * (g_unit - m1 - unit * m2)
    cell_rows = mm(pick[...], cell.astype(BF16), NT).astype(BF16)
    for q in range(GY):
        send[q, 0 : SIN * PIECE, :] = cell_rows[q * 32 : (q + 1) * 32]


def gather_kernel(
    scale, at, r0, r1, r2, r3, grad_in, grad_out, grad_slice, flat, tail, sem
):
    y, core, x = at[0], at[1], at[2]
    for dy, recv in enumerate((r0, r1, r2, r3)):
        for dx in range(4):
            for dc in range(2):
                index = (((y - dy) & 3) * 2 + (core ^ dc)) * 4 + ((x - dx) & 3)
                start = pl.multiple_of(index * GRAD_ROWS, 8)
                flat[pl.ds(start, GRAD_ROWS), :] = recv[dx * 2 + dc].astype(F32) * scale
    tail[...] = flat[6 * C : 6 * C + WIDTH, 0:SLICES]
    copies = []
    for b in range(6):
        out, c = (grad_in, b) if b < 4 else (grad_out, b - 4)
        target = out.at[:, c * 128 : (c + 1) * 128]
        copies.append(pltpu.make_async_copy(flat.at[b * C : (b + 1) * C], target, sem.at[b]))
    copies.append(pltpu.make_async_copy(tail, grad_slice, sem.at[6]))
    for copy in copies:
        copy.start()
    for copy in copies:
        copy.wait()


def unpack_kernel(home, result, cell_grad, cells, rows, sem):
    copies = []
    order = piece_order(True)
    for j in range(8):
        got = jnp.concatenate([home[4 * j + a] for a in range(4)], axis=0)
        moved = mm(order, got).astype(BF16)
        span = pl.ds(16 * j, 16)
        cells[:, span, :] = moved[0 : SIN * 16].reshape(SIN, 16, C)
        rows[:, span, :] = moved[SIN * 16 :].reshape(SOUT, 16, C)
        if j % 2 == 1:
            both = pl.ds(16 * (j - 1), 32)
            pair = [
                pltpu.make_async_copy(cells.at[:, both, :], cell_grad.at[:, both, :], sem.at[j - 1]),
                pltpu.make_async_copy(rows.at[:, both, :], result.at[:, both, :], sem.at[j]),
            ]
            for copy in pair:
                copy.start()
            copies += pair
    for copy in copies:
        copy.wait()


def shards(
    cells, tally, plan, cot, gain, entrance, portion, softness, base,
    request, lookup, content, exit_w,
):
    gain = gain.reshape(1, C)
    softness = softness.reshape(1, WIDTH)
    base = base.reshape(1, HEADS)
    scale = 1.0 / math.sqrt(GX * GY * SIN * BLK)

    def swap(x, axes):
        return lax.all_to_all(x, axes, 0, 0, tiled=True)

    def shifted(x, axis, n, d):
        return lax.ppermute(x, axis, [(i, (i + d) % n) for i in range(n)])

    sent = call(
        pack_kernel,
        sds((GY, TALL, 128), BF16),
        tally, plan, cells.reshape(SIN, BLK, C), cot.reshape(SOUT, BLK, C),
        scalars=2,
        hbm_out=True,
        vmem=62,
        scratch=[
            pltpu.VMEM((GY, TALL, 128), BF16),
            pltpu.SemaphoreType.DMA((8,)),
        ],
    )
    entrance_t, exit_t, spread, soft_spread, gain_col, base_col, soft_col = call(
        weight_kernel,
        [
            sds((2 * C, C), BF16),
            sds((C, C), BF16),
            sds((C, 512), BF16),
            sds((16, C), BF16),
            sds((C, 128), F32),
            sds((HEADS, 128), F32),
            sds((WIDTH, 128), F32),
        ],
        gain, entrance, portion, softness, base, exit_w,
    )
    recv = swap(sent, ("z", "x"))
    spot = (lax.axis_index("z") * 4 + lax.axis_index("x")).astype(jnp.int32).reshape(1)
    state = call(
        forward_kernel,
        [
            sds((HEADS, TOKEN_ROWS, 128), BF16),
            sds((HOME, ROWS), BF16),
            sds((C, ROWS), BF16),
            sds((C, ROWS), BF16),
            sds((2 * C, ROWS), BF16),
            sds((512, ROWS), F32),
            sds((512, ROWS), F32),
            sds((512, ROWS), BF16),
            sds((C, ROWS), BF16),
            sds((C, ROWS), BF16),
            sds((8, ROWS), F32),
            sds((16, ROWS), F32),
        ],
        spot, recv, entrance_t, exit_w, spread, soft_spread, gain_col, base_col,
        scalars=1,
    )
    token, saved = state[0], state[1:]
    token = swap(token, ("y", "core"))
    token = swap(spread_sum(token, GY, BF16), ("z", "x"))
    mix = call(
        token_kernel, sds((GX, MIX_ROWS, 128), BF16), token, request, lookup, content
    )
    mix = swap(mix, ("y", "core"))
    send, grads = call(
        backward_kernel,
        [sds((GY, SEND, C), BF16), sds((GY * GRAD_ROWS, 128), BF16)],
        mix, entrance, exit_t, spread, gain_col, soft_col, *saved,
        scratch=[
            pltpu.VMEM((2 * C + 16, 512), BF16),
            pltpu.VMEM((2 * C + 16, ROWS), BF16),
            pltpu.VMEM((512, ROWS), F32),
            pltpu.VMEM((512, ROWS), BF16),
            pltpu.VMEM((2 * C, ROWS), BF16),
        ],
    )
    grads = swap(grads.reshape(GY, GRAD_ROWS, 128), ("y", "core", "x"))
    grads = swap(spread_sum(grads, 8, BF16), ("z",))
    grads = spread_sum(grads, 1, BF16)
    send, grads = lax.optimization_barrier((send, grads))
    home = swap(send, ("z", "x"))
    grads = jnp.concatenate([grads, shifted(grads, "core", 2, 1)], axis=0)
    grads = jnp.concatenate([grads] + [shifted(grads, "x", 4, d) for d in (1, 2, 3)], axis=0)
    gathered = [grads] + [shifted(grads, "y", 4, d) for d in (1, 2, 3)]
    at = jnp.stack([lax.axis_index(a) for a in ("y", "core", "x")]).astype(jnp.int32)
    result, cell_grad = call(
        unpack_kernel,
        [sds((SOUT, BLK, C), BF16), sds((SIN, BLK, C), BF16)],
        home,
        hbm_out=True,
        scratch=[
            pltpu.VMEM((SIN, BLK, C), BF16),
            pltpu.VMEM((SOUT, BLK, C), BF16),
            pltpu.SemaphoreType.DMA((8,)),
        ],
    )
    grad_in, grad_out, grad_slice = call(
        lambda *refs: gather_kernel(scale, *refs),
        [sds((C, 2 * C), F32), sds((C, C), F32), sds((WIDTH, SLICES), F32)],
        at, *gathered,
        scalars=1,
        hbm_out=True,
        scratch=[
            pltpu.VMEM((GY * GRAD_ROWS, 128), F32),
            pltpu.VMEM((WIDTH, SLICES), F32),
            pltpu.SemaphoreType.DMA((7,)),
        ],
    )
    result = result.reshape(SOUT * BLK, C)
    cell_grad = cell_grad.reshape(SIN * BLK, C)
    return result, cell_grad, grad_in, grad_out, grad_slice


def solution(mesh):
    grid = Mesh(mesh.devices.reshape(4, 2, 8, 4), ("y", "core", "z", "x"))
    whole = ("y", "core", "z", "x")
    placed = (P(whole, None), P(whole), P(whole, None), P(whole, None)) + (P(),) * 9
    return jax.shard_map(
        shards,
        mesh=grid,
        in_specs=placed,
        out_specs=(P(whole, None), P(whole, None), P(), P(), P()),
        check_vma=False,
    )
```
